32 devices in a mesh: win: 8 (over y, x, core), row: 4 (over z).
Axes of the slice: x: 2, y: 2, z: 4, core: 2. Of those that a mesh axis runs over, the one named last changes fastest.
Arguments:
- downgoing: float32 [8, 3072, 3072], P('win', 'row'), may hold values from -64 to 64
- upgoing: float32 [8, 64, 3072], P('win'), may hold values from -6 to 6
Outputs:
- filters: float32 [32, 2, 64, 3072], P('win', None, None, 'row')
The draws below stay inside these ranges and needn't reach their ends.
All inputs are finite; a program needn't handle non-finite values.
Results may differ from the reference program's by a relative error of at most 0.00016.
Values sent between devices are 32-bit elements; how exact they have to be, the bound alone decides.
A program may use at most 128 MiB of HBM per device.

```python
import math
import jax
import jax.numpy as jnp
from jax import lax

NCH = 3072
NT = 3072
NVS = 64
ITERS = 2
NWT = 8
NF = 32


def draw_downgoing(key, part):
    key_win, key_chan, key_noise = jax.random.split(key, 3)
    win_gain = jnp.exp(jax.random.uniform(key_win, (NWT, 1, 1), jnp.float32, -1.15, 1.15))
    chan_gain = jnp.exp(jax.random.uniform(key_chan, (1, NCH, 1), jnp.float32, -1.15, 1.15))
    ramp_gain = jnp.exp(0.55 * jnp.arange(NCH, dtype=jnp.float32) / NCH).reshape(1, NCH, 1)
    noise = jax.random.normal(key_noise, (NWT, NCH, NT), jnp.float32)
    return jnp.clip(noise * win_gain * chan_gain * ramp_gain, -64.0, 64.0)


def block_levels(rng, shape, shards, least, top_value):
    level, own = 1.0, jax.random.fold_in(rng, 6)
    for dim, shards_of in shards:
        draws = jnp.exp(jax.random.uniform(jax.random.fold_in(own, dim), (shards_of,), jnp.float32, least / len(shards), top_value / len(shards)))
        level = level * jnp.repeat(draws, shape[dim] // shards_of).reshape([-1 if axis == dim else 1 for axis in range(len(shape))])
    return level


def centred(stream_key, shape, scale, bound, shards=(), kind=jnp.bfloat16):
    loudness = block_levels(stream_key, shape, shards, -0.22, 0.18) if shards else 1.0
    array = jax.random.normal(stream_key, shape, jnp.float32) * scale * loudness
    return jnp.minimum(jnp.maximum(array, -bound), bound).astype(kind)


def setup_inputs(seed: int = 0) -> dict:
    arg_keys = jax.random.split(jax.random.key(seed), 3)
    return {
        "downgoing": draw_downgoing(jax.random.fold_in(arg_keys[2], 71), 0),
        "upgoing": centred(arg_keys[1], (NWT, NVS, NT), 1.0, 6.0, ((0, 8),), jnp.float32),
    }


damping = 0.5

def exact_dot(first, second):
    return jnp.dot(first, second, precision=lax.Precision.HIGHEST, preferred_element_type=jnp.float32)

def dft_table(n_samples, n_bins):
    sample_idx = jnp.arange(n_samples, dtype=jnp.int32)
    bin_idx = jnp.arange(1, n_bins + 1, dtype=jnp.int32)
    angles = (sample_idx[:, None] * bin_idx[None, :] % n_samples).astype(jnp.float32) * (2.0 * math.pi / n_samples)
    return jnp.concatenate([jnp.cos(angles), -jnp.sin(angles)], axis=1) * (1.0 / math.sqrt(n_samples))

def spectra(series, basis, n_bins):

    def one_window(window):
        return exact_dot(basis.T, window.T)
    flat = lax.map(one_window, series)
    return flat.reshape(series.shape[0], 2, n_bins, series.shape[1])

def solve_bin(down_re, down_im, up_re, up_im):
    n_chan = down_re.shape[1]
    root_chan = math.sqrt(n_chan)
    rhs_re = (exact_dot(up_re.T, down_re) + exact_dot(up_im.T, down_im)) / root_chan
    rhs_im = (exact_dot(up_im.T, down_re) - exact_dot(up_re.T, down_im)) / root_chan

    def operate(dir_re, dir_im):
        sum_re = exact_dot(dir_re, down_re.T) - exact_dot(dir_im, down_im.T)
        sum_im = exact_dot(dir_re, down_im.T) + exact_dot(dir_im, down_re.T)
        img_re = (exact_dot(sum_re, down_re) + exact_dot(sum_im, down_im)) / n_chan + damping * dir_re
        img_im = (exact_dot(sum_im, down_re) - exact_dot(sum_re, down_im)) / n_chan + damping * dir_im
        return (img_re, img_im)
    filt_re = jnp.zeros_like(rhs_re)
    filt_im = jnp.zeros_like(rhs_im)
    res_re, res_im = (rhs_re, rhs_im)
    dir_re, dir_im = (rhs_re, rhs_im)
    norm_old = lax.optimization_barrier(jnp.sum(res_re * res_re + res_im * res_im, axis=-1, keepdims=True))
    for iteration in range(ITERS):
        img_re, img_im = operate(dir_re, dir_im)
        curvature = lax.optimization_barrier(jnp.sum(dir_re * img_re + dir_im * img_im, axis=-1, keepdims=True))
        step_size = norm_old / curvature
        filt_re = filt_re + step_size * dir_re
        filt_im = filt_im + step_size * dir_im
        res_re = res_re - step_size * img_re
        res_im = res_im - step_size * img_im
        norm_new = lax.optimization_barrier(jnp.sum(res_re * res_re + res_im * res_im, axis=-1, keepdims=True))
        ratio = norm_new / norm_old
        dir_re = res_re + ratio * dir_re
        dir_im = res_im + ratio * dir_im
        norm_old = norm_new
    out_scale = math.sqrt(n_chan / down_re.shape[0])
    return jnp.stack([filt_re, filt_im]) * out_scale

def reference(downgoing, upgoing):
    basis = dft_table(NT, NF)
    spec_down = spectra(downgoing, basis, NF)
    spec_up = spectra(upgoing, basis, NF)
    by_bin = (jnp.moveaxis(spec_down, 2, 0), jnp.moveaxis(spec_up, 2, 0))

    def one_bin(pair_bin):
        return solve_bin(pair_bin[0][:, 0], pair_bin[0][:, 1], pair_bin[1][:, 0], pair_bin[1][:, 1])
    return lax.map(one_bin, by_bin)
```

```python
import functools
import math

import jax
import jax.numpy as jnp
import numpy as np
from jax import lax
from jax.experimental import pallas as pl
from jax.experimental.pallas import tpu as pltpu
from jax.sharding import PartitionSpec as P

FREQ_DEV = 4
ITERS = 2
DAMPING = 0.5
LANES = 128
MESH = pl.DeviceIdType.MESH
F32, BF16 = jnp.float32, jnp.bfloat16


def dft_table(n_samples, n_bins):
    angles = (np.arange(n_samples)[:, None] * np.arange(1, n_bins + 1)[None, :] % n_samples) * (
        2.0 * math.pi / n_samples
    )
    table = np.stack([np.cos(angles), -np.sin(angles)], axis=2).reshape(n_samples, 2 * n_bins)
    table = (table / math.sqrt(n_samples)).astype(np.float32)
    head = table.astype(BF16)
    tail = (table - head.astype(np.float32)).astype(BF16)
    return np.concatenate([head, tail], axis=1)


def halves(value):
    head = value.astype(BF16)
    return head, (value - head.astype(F32)).astype(BF16)


def dot(first, second, dims):
    return lax.dot_general(first, second, (dims, ((), ())), preferred_element_type=F32)


def spectra(series, table):
    m, n_samples = series.shape
    step = 256
    total = None
    for at in range(0, n_samples, step):
        head, tail = halves(series[:, at : at + step])
        part = dot(jnp.concatenate([head, tail], axis=0), table[at : at + step, :], ((1,), (0,)))
        part = part[:m] + part[m:]
        total = part if total is None else total + part
    if m % LANES:
        total = jnp.concatenate([total, jnp.zeros((LANES - m % LANES, total.shape[1]), F32)], axis=0)
    total = total.T
    n = total.shape[0] // 2
    return total[:n] + total[n:]


def solve(rhs, gram, n_freq, n_chan, scale):
    rows, n_virt = rhs.shape

    head, tail = halves(gram)
    operator = jnp.concatenate([head, head, tail], axis=1)

    def project(coef):
        c_head, c_tail = halves(coef)
        return dot(operator, jnp.concatenate([c_head, c_tail, c_head], axis=0), ((1,), (0,)))

    def inner(one, two):
        prod = (one * two).reshape(n_freq, rows // n_freq, n_virt)
        total = jnp.sum(prod, axis=1, keepdims=True)
        return jnp.broadcast_to(total, prod.shape).reshape(rows, n_virt)

    filt = jnp.zeros_like(rhs)
    resid, direc = rhs, rhs
    resid_g = project(resid)
    direc_g = resid_g
    norm_old = inner(resid, resid_g)
    for iteration in range(ITERS):
        image = direc_g / n_chan + DAMPING * direc
        curvature = inner(direc_g, image)
        step = norm_old / curvature
        filt = filt + step * direc
        if iteration + 1 < ITERS:
            resid = resid - step * image
            resid_g = resid_g - step * project(image)
            norm_new = inner(resid, resid_g)
            ratio = norm_new / norm_old
            direc = resid + ratio * direc
            direc_g = resid_g + ratio * direc_g
            norm_old = norm_new
    return filt * scale


def solve_kernel(
    dims, x_hbm, up_hbm, tab_hbm, eh_out, el_out, y_out,
    xv, upv, tab, sbuf, ubuf, recv, urecv, eh, el, g_send, g_recv,
    in_sem, send_sem, recv_sem, g_sem, out_sem,
):
    n_win, n_row, n_chunk, width, n_virt, n_chan = dims
    slab = 2 * FREQ_DEV
    rows = n_win * slab
    block = 2 * n_win
    me, row = lax.axis_index("win"), lax.axis_index("row")

    loads = [
        pltpu.make_async_copy(tab_hbm, tab, in_sem.at[0]),
        pltpu.make_async_copy(up_hbm.at[0], upv, in_sem.at[1]),
    ]
    for ch in range(n_chunk):
        loads.append(
            pltpu.make_async_copy(
                x_hbm.at[0, pl.ds(ch * width, width), :], xv.at[ch], in_sem.at[2 + ch]
            )
        )
    for load in loads:
        load.start()

    win_peers = [lax.rem(me + off, n_win) for off in range(1, n_win)]
    row_peers = [lax.rem(row + off, n_row) for off in range(1, n_row)]
    barrier = pltpu.get_barrier_semaphore()
    for peer in win_peers:
        pl.semaphore_signal(barrier, inc=1, device_id={"win": peer}, device_id_type=MESH)
    for peer in row_peers:
        pl.semaphore_signal(barrier, inc=1, device_id={"row": peer}, device_id_type=MESH)

    def share(src, dst, at):
        own = pl.ds(pl.multiple_of(me * slab, slab), slab)
        dst[:, own, :] = src[:, own, :]
        for peer in win_peers:
            pltpu.make_async_remote_copy(
                src_ref=src.at[:, pl.ds(pl.multiple_of(peer * slab, slab), slab), :],
                dst_ref=dst.at[:, own, :],
                send_sem=send_sem.at[at],
                recv_sem=recv_sem.at[at],
                device_id={"win": peer},
                device_id_type=MESH,
            ).start()

    def put(dst, value):
        for sub in range(dst.shape[0]):
            dst[sub] = value[:, sub * LANES : (sub + 1) * LANES]

    def gather(src, number):
        parts = [src[sub, pl.ds(number, n_win, stride=slab), :] for sub in range(src.shape[0])]
        return jnp.concatenate(parts, axis=1) if len(parts) > 1 else parts[0]

    def await_all(ref, sem):
        part = ref.at[:, pl.ds(0, (n_win - 1) * slab), :]
        pltpu.make_async_copy(part, part, sem).wait()

    loads[0].wait()
    loads[1].wait()
    put(ubuf, spectra(upv, tab))
    pl.semaphore_wait(barrier, n_win + n_row - 2)
    share(ubuf, urecv, n_chunk)
    for ch in range(n_chunk):
        loads[2 + ch].wait()
        put(sbuf.at[ch], spectra(xv.at[ch], tab))
        share(sbuf.at[ch], recv.at[ch], ch)

    gram = None
    stores = []
    for ch in range(n_chunk):
        await_all(recv.at[ch], recv_sem.at[ch])
        left, right = [], []
        for f in range(FREQ_DEV):
            real = gather(recv.at[ch], 2 * f)
            imag = gather(recv.at[ch], 2 * f + 1)
            left += [real, imag]
            right += [-imag, real]
        ext = jnp.concatenate(
            [jnp.concatenate(left, axis=0), jnp.concatenate(right, axis=0)], axis=1
        )
        head, tail = halves(ext)
        eh[ch] = head
        el[ch] = tail
        for number, (src, dst) in enumerate(((eh, eh_out), (el, el_out))):
            store = pltpu.make_async_copy(src.at[ch], dst.at[ch], out_sem.at[2 * ch + number])
            store.start()
            stores.append(store)
        part = dot(
            jnp.concatenate([head, head, tail], axis=1),
            jnp.concatenate([head, tail, head], axis=1),
            ((1,), (1,)),
        )
        gram = part if gram is None else gram + part

    row_id = lax.broadcasted_iota(jnp.int32, (rows, rows), 0) // block
    col_id = lax.broadcasted_iota(jnp.int32, (rows, rows), 1) // block
    same_bin = row_id == col_id
    gram = jnp.where(same_bin, gram, 0.0)
    folded = gram[:block]
    for f in range(1, FREQ_DEV):
        folded = folded + gram[f * block : (f + 1) * block]
    packed = 2 * rows <= LANES
    if packed:
        folded = jnp.concatenate([folded[:n_win], folded[n_win:]], axis=1)
    g_send[...] = folded
    g_recv[row] = folded
    for off, peer in enumerate(row_peers):
        pltpu.make_async_remote_copy(
            src_ref=g_send,
            dst_ref=g_recv.at[row],
            send_sem=g_sem.at[0],
            recv_sem=g_sem.at[1],
            device_id={"row": peer},
            device_id_type=MESH,
        ).start()
    await_all(urecv, recv_sem.at[n_chunk])
    rhs = jnp.concatenate(
        [gather(urecv, number) for number in range(slab)], axis=0
    ) / math.sqrt(n_chan)
    rhs = rhs[:, :n_virt]
    if n_row > 1:
        part = g_recv.at[pl.ds(0, n_row - 1)]
        pltpu.make_async_copy(part, part, g_sem.at[1]).wait()
    folded = g_recv[0]
    for other in range(1, n_row):
        folded = folded + g_recv[other]
    if packed:
        folded = jnp.concatenate([folded[:, :rows], folded[:, rows:]], axis=0)
    gram = jnp.where(same_bin, jnp.concatenate([folded] * FREQ_DEV, axis=0), 0.0)
    y_out[...] = solve(rhs, gram, FREQ_DEV, n_chan, math.sqrt(n_chan / n_win))

    if n_row > 1:
        part = g_recv.at[pl.ds(0, n_row - 1)]
        pltpu.make_async_copy(part, part, g_sem.at[0]).wait()
    for ch in range(n_chunk):
        await_all(recv.at[ch], send_sem.at[ch])
    await_all(urecv, send_sem.at[n_chunk])
    for store in stores:
        store.wait()


def expand_kernel(dims, eh, el, y, out_hbm, ov, sem):
    n_win, n_chunk, width, n_virt = dims
    block = 2 * n_win
    stores = []
    for f in range(FREQ_DEV):
        own = slice(f * block, (f + 1) * block)
        head, tail = halves(y[own, :])
        coef = jnp.concatenate([head, tail, head], axis=0)
        for ch in range(n_chunk):
            big = eh[ch, own, :]
            part = dot(coef, jnp.concatenate([big, big, el[ch, own, :]], axis=0), ((0,), (0,)))
            span = slice(ch * width, (ch + 1) * width)
            ov[f, 0, :, span] = part[:, :width]
            ov[f, 1, :, span] = part[:, width:]
        store = pltpu.make_async_copy(ov.at[f], out_hbm.at[f], sem.at[f])
        store.start()
        stores.append(store)
    for store in stores:
        store.wait()


def body(downgoing, upgoing):
    _, n_local, n_samples = downgoing.shape
    n_virt = upgoing.shape[1]
    n_win, n_row = lax.axis_size("win"), lax.axis_size("row")
    n_chan = n_local * n_row
    width = 256 if n_local % 256 == 0 else 128
    n_chunk = n_local // width
    slab = 2 * FREQ_DEV
    rows = n_win * slab
    block = 2 * n_win
    table = jnp.asarray(dft_table(n_samples, FREQ_DEV * n_win))
    g_shape = (n_win, 2 * rows) if 2 * rows <= LANES else (block, rows)
    v_pad = -(-n_virt // LANES) * LANES
    dims = (n_win, n_row, n_chunk, width, n_virt, n_chan)
    any_spec = pl.BlockSpec(memory_space=pl.ANY)
    vmem_spec = pl.BlockSpec(memory_space=pltpu.VMEM)
    ext = jax.ShapeDtypeStruct((n_chunk, rows, 2 * width), BF16)
    eh, el, y = pl.pallas_call(
        functools.partial(solve_kernel, dims),
        out_shape=(ext, ext, jax.ShapeDtypeStruct((rows, n_virt), F32)),
        in_specs=[any_spec] * 3,
        out_specs=(any_spec, any_spec, vmem_spec),
        scratch_shapes=[
            pltpu.VMEM((n_chunk, width, n_samples), F32),
            pltpu.VMEM((n_virt, n_samples), F32),
            pltpu.VMEM(table.shape, BF16),
            pltpu.VMEM((n_chunk, width // LANES, rows, LANES), F32),
            pltpu.VMEM((v_pad // LANES, rows, LANES), F32),
            pltpu.VMEM((n_chunk, width // LANES, rows, LANES), F32),
            pltpu.VMEM((v_pad // LANES, rows, LANES), F32),
            pltpu.VMEM((n_chunk, rows, 2 * width), BF16),
            pltpu.VMEM((n_chunk, rows, 2 * width), BF16),
            pltpu.VMEM(g_shape, F32),
            pltpu.VMEM((n_row,) + g_shape, F32),
            pltpu.SemaphoreType.DMA((2 + n_chunk,)),
            pltpu.SemaphoreType.DMA((n_chunk + 1,)),
            pltpu.SemaphoreType.DMA((n_chunk + 1,)),
            pltpu.SemaphoreType.DMA((2,)),
            pltpu.SemaphoreType.DMA((2 * n_chunk,)),
        ],
        compiler_params=pltpu.CompilerParams(
            collective_id=0, has_side_effects=True, vmem_limit_bytes=50 * 1024 * 1024
        ),
        name="solve_bins",
    )(downgoing, upgoing, table)
    out_shape = (FREQ_DEV, 2, n_virt, n_local)
    return pl.pallas_call(
        functools.partial(expand_kernel, (n_win, n_chunk, width, n_virt)),
        out_shape=jax.ShapeDtypeStruct(out_shape, F32),
        in_specs=[vmem_spec] * 3,
        out_specs=any_spec,
        scratch_shapes=[pltpu.VMEM(out_shape, F32), pltpu.SemaphoreType.DMA((FREQ_DEV,))],
        compiler_params=pltpu.CompilerParams(vmem_limit_bytes=50 * 1024 * 1024),
        name="expand_bins",
    )(eh, el, y)


def solution(mesh):
    in_specs = (P("win", "row", None), P("win", None, None))
    out_specs = P("win", None, None, "row")
    return jax.shard_map(body, mesh=mesh, in_specs=in_specs, out_specs=out_specs, check_vma=False)
```

```python
import functools
import math

import jax
import jax.numpy as jnp
import numpy as np
from jax import lax
from jax.experimental import pallas as pl
from jax.experimental.pallas import tpu as pltpu
from jax.sharding import PartitionSpec as P

FREQ_DEV = 4
PIECE = 1024
AHEAD = 4
ITERS = 2
DAMPING = 0.5
LANES = 128
MESH = pl.DeviceIdType.MESH
F32, BF16 = jnp.float32, jnp.bfloat16


def dft_table(n_samples, n_bins):
    angles = (np.arange(n_samples)[:, None] * np.arange(1, n_bins + 1)[None, :] % n_samples) * (
        2.0 * math.pi / n_samples
    )
    table = np.stack([np.cos(angles), -np.sin(angles)], axis=2).reshape(n_samples, 2 * n_bins)
    table = (table / math.sqrt(n_samples)).astype(np.float32)
    head = table.astype(BF16)
    tail = (table - head.astype(np.float32)).astype(BF16)
    return np.concatenate([head, tail], axis=1)


def halves(value):
    head = value.astype(BF16)
    return head, (value - head.astype(F32)).astype(BF16)


def dot(first, second, dims):
    return lax.dot_general(first, second, (dims, ((), ())), preferred_element_type=F32)


def accumulate(total, series, table):
    m = series.shape[0]
    head, tail = halves(series)
    part = dot(jnp.concatenate([head, tail], axis=0), table, ((1,), (0,)))
    part = part[:m] + part[m:]
    return part if total is None else total + part


def by_bin(total):
    m = total.shape[0]
    if m % LANES:
        total = jnp.concatenate([total, jnp.zeros((LANES - m % LANES, total.shape[1]), F32)], axis=0)
    total = total.T
    n = total.shape[0] // 2
    return total[:n] + total[n:]


def solve(rhs, gram, n_freq, n_chan, scale):
    rows, n_virt = rhs.shape

    head, tail = halves(gram)
    operator = jnp.concatenate([head, head, tail], axis=1)

    def project(coef):
        c_head, c_tail = halves(coef)
        return dot(operator, jnp.concatenate([c_head, c_tail, c_head], axis=0), ((1,), (0,)))

    def inner(one, two):
        prod = (one * two).reshape(n_freq, rows // n_freq, n_virt)
        total = jnp.sum(prod, axis=1, keepdims=True)
        return jnp.broadcast_to(total, prod.shape).reshape(rows, n_virt)

    filt = jnp.zeros_like(rhs)
    resid, direc = rhs, rhs
    resid_g = project(resid)
    direc_g = resid_g
    norm_old = inner(resid, resid_g)
    for iteration in range(ITERS):
        image = direc_g / n_chan + DAMPING * direc
        curvature = inner(direc_g, image)
        step = norm_old / curvature
        filt = filt + step * direc
        if iteration + 1 < ITERS:
            resid = resid - step * image
            resid_g = resid_g - step * project(image)
            norm_new = inner(resid, resid_g)
            ratio = norm_new / norm_old
            direc = resid + ratio * direc
            direc_g = resid_g + ratio * direc_g
            norm_old = norm_new
    return filt * scale


def solve_kernel(
    dims, x_hbm, up_hbm, tab_hbm, eh_out, el_out, y_out,
    xv, upv, tab, sbuf, ubuf, recv, urecv, eh, el, g_send, g_recv,
    in_sem, send_sem, recv_sem, g_sem, out_sem,
):
    n_win, n_row, n_chunk, width, n_virt, n_chan = dims
    slab = 2 * FREQ_DEV
    rows = n_win * slab
    block = 2 * n_win
    me, row = lax.axis_index("win"), lax.axis_index("row")

    n_piece, piece = tab.shape[0], tab.shape[1]
    loads, ready = [], []
    for ch in range(n_chunk):
        for k in range(n_piece):
            span = pl.ds(k * piece, piece)
            pairs = [(x_hbm.at[0, pl.ds(ch * width, width), span], xv.at[ch, k])]
            if ch == 0:
                pairs = [(tab_hbm.at[span, :], tab.at[k]), (up_hbm.at[0, :, span], upv.at[k])] + pairs
            for src, dst in pairs:
                loads.append(pltpu.make_async_copy(src, dst, in_sem.at[len(loads)]))
            ready.append(len(loads))
    ahead = 3 * AHEAD
    for load in loads[:ahead]:
        load.start()
    taken = [0]

    def await_piece(number):
        for at in range(taken[0], ready[number]):
            loads[at].wait()
        started = ahead + taken[0]
        taken[0] = ready[number]
        for load in loads[started : ahead + taken[0]]:
            load.start()

    win_peers = [lax.rem(me + off, n_win) for off in range(1, n_win)]
    row_peers = [lax.rem(row + off, n_row) for off in range(1, n_row)]
    barrier = pltpu.get_barrier_semaphore()
    for peer in win_peers:
        pl.semaphore_signal(barrier, inc=1, device_id={"win": peer}, device_id_type=MESH)
    for peer in row_peers:
        pl.semaphore_signal(barrier, inc=1, device_id={"row": peer}, device_id_type=MESH)

    def share(src, dst, at):
        own = pl.ds(pl.multiple_of(me * slab, slab), slab)
        dst[:, own, :] = src[:, own, :]
        for peer in win_peers:
            pltpu.make_async_remote_copy(
                src_ref=src.at[:, pl.ds(pl.multiple_of(peer * slab, slab), slab), :],
                dst_ref=dst.at[:, own, :],
                send_sem=send_sem.at[at],
                recv_sem=recv_sem.at[at],
                device_id={"win": peer},
                device_id_type=MESH,
            ).start()

    def put(dst, value):
        for sub in range(dst.shape[0]):
            dst[sub] = value[:, sub * LANES : (sub + 1) * LANES]

    def gather(src, number):
        parts = [src[sub, pl.ds(number, n_win, stride=slab), :] for sub in range(src.shape[0])]
        return jnp.concatenate(parts, axis=1) if len(parts) > 1 else parts[0]

    def await_all(ref, sem):
        part = ref.at[:, pl.ds(0, (n_win - 1) * slab), :]
        pltpu.make_async_copy(part, part, sem).wait()

    for ch in range(n_chunk):
        total = None
        for k in range(n_piece):
            await_piece(ch * n_piece + k)
            series = xv[ch, k]
            if ch == 0:
                series = jnp.concatenate([series, upv[k]], axis=0)
            total = accumulate(total, series, tab[k])
        put(sbuf.at[ch], by_bin(total[:width]))
        if ch == 0:
            put(ubuf, by_bin(total[width:]))
            pl.semaphore_wait(barrier, n_win + n_row - 2)
        share(sbuf.at[ch], recv.at[ch], ch)
        if ch == 0:
            share(ubuf, urecv, n_chunk)

    gram = None
    stores = []
    for ch in range(n_chunk):
        await_all(recv.at[ch], recv_sem.at[ch])
        left, right = [], []
        for f in range(FREQ_DEV):
            real = gather(recv.at[ch], 2 * f)
            imag = gather(recv.at[ch], 2 * f + 1)
            left += [real, imag]
            right += [-imag, real]
        ext = jnp.concatenate(
            [jnp.concatenate(left, axis=0), jnp.concatenate(right, axis=0)], axis=1
        )
        head, tail = halves(ext)
        eh[ch] = head
        el[ch] = tail
        for number, (src, dst) in enumerate(((eh, eh_out), (el, el_out))):
            store = pltpu.make_async_copy(src.at[ch], dst.at[ch], out_sem.at[2 * ch + number])
            store.start()
            stores.append(store)
        part = dot(
            jnp.concatenate([head, head, tail], axis=1),
            jnp.concatenate([head, tail, head], axis=1),
            ((1,), (1,)),
        )
        gram = part if gram is None else gram + part

    row_id = lax.broadcasted_iota(jnp.int32, (rows, rows), 0) // block
    col_id = lax.broadcasted_iota(jnp.int32, (rows, rows), 1) // block
    same_bin = row_id == col_id
    gram = jnp.where(same_bin, gram, 0.0)
    folded = gram[:block]
    for f in range(1, FREQ_DEV):
        folded = folded + gram[f * block : (f + 1) * block]
    packed = 2 * rows <= LANES
    if packed:
        folded = jnp.concatenate([folded[:n_win], folded[n_win:]], axis=1)
    g_send[...] = folded
    g_recv[row] = folded
    for off, peer in enumerate(row_peers):
        pltpu.make_async_remote_copy(
            src_ref=g_send,
            dst_ref=g_recv.at[row],
            send_sem=g_sem.at[0],
            recv_sem=g_sem.at[1],
            device_id={"row": peer},
            device_id_type=MESH,
        ).start()
    await_all(urecv, recv_sem.at[n_chunk])
    rhs = jnp.concatenate(
        [gather(urecv, number) for number in range(slab)], axis=0
    ) / math.sqrt(n_chan)
    rhs = rhs[:, :n_virt]
    if n_row > 1:
        part = g_recv.at[pl.ds(0, n_row - 1)]
        pltpu.make_async_copy(part, part, g_sem.at[1]).wait()
    folded = g_recv[0]
    for other in range(1, n_row):
        folded = folded + g_recv[other]
    if packed:
        folded = jnp.concatenate([folded[:, :rows], folded[:, rows:]], axis=0)
    gram = jnp.where(same_bin, jnp.concatenate([folded] * FREQ_DEV, axis=0), 0.0)
    y_out[...] = solve(rhs, gram, FREQ_DEV, n_chan, math.sqrt(n_chan / n_win))

    if n_row > 1:
        part = g_recv.at[pl.ds(0, n_row - 1)]
        pltpu.make_async_copy(part, part, g_sem.at[0]).wait()
    for ch in range(n_chunk):
        await_all(recv.at[ch], send_sem.at[ch])
    await_all(urecv, send_sem.at[n_chunk])
    for store in stores:
        store.wait()


def expand_kernel(dims, eh, el, y, out_hbm, ov, sem):
    n_win, n_chunk, width, n_virt = dims
    block = 2 * n_win
    stores = []
    for f in range(FREQ_DEV):
        own = slice(f * block, (f + 1) * block)
        head, tail = halves(y[own, :])
        coef = jnp.concatenate([head, tail, head], axis=0)
        for ch in range(n_chunk):
            big = eh[ch, own, :]
            part = dot(coef, jnp.concatenate([big, big, el[ch, own, :]], axis=0), ((0,), (0,)))
            span = slice(ch * width, (ch + 1) * width)
            ov[f, 0, :, span] = part[:, :width]
            ov[f, 1, :, span] = part[:, width:]
        store = pltpu.make_async_copy(ov.at[f], out_hbm.at[f], sem.at[f])
        store.start()
        stores.append(store)
    for store in stores:
        store.wait()


def body(downgoing, upgoing):
    _, n_local, n_samples = downgoing.shape
    n_virt = upgoing.shape[1]
    n_win, n_row = lax.axis_size("win"), lax.axis_size("row")
    n_chan = n_local * n_row
    width = 256 if n_local % 256 == 0 else 128
    n_chunk = n_local // width
    piece = PIECE if n_samples % PIECE == 0 else n_samples
    n_piece = n_samples // piece
    slab = 2 * FREQ_DEV
    rows = n_win * slab
    block = 2 * n_win
    table = jnp.asarray(dft_table(n_samples, FREQ_DEV * n_win))
    g_shape = (n_win, 2 * rows) if 2 * rows <= LANES else (block, rows)
    v_pad = -(-n_virt // LANES) * LANES
    dims = (n_win, n_row, n_chunk, width, n_virt, n_chan)
    any_spec = pl.BlockSpec(memory_space=pl.ANY)
    vmem_spec = pl.BlockSpec(memory_space=pltpu.VMEM)
    ext = jax.ShapeDtypeStruct((n_chunk, rows, 2 * width), BF16)
    eh, el, y = pl.pallas_call(
        functools.partial(solve_kernel, dims),
        out_shape=(ext, ext, jax.ShapeDtypeStruct((rows, n_virt), F32)),
        in_specs=[pl.BlockSpec(memory_space=pltpu.MemorySpace.HBM)] * 3,
        out_specs=(any_spec, any_spec, vmem_spec),
        scratch_shapes=[
            pltpu.VMEM((n_chunk, n_piece, width, piece), F32),
            pltpu.VMEM((n_piece, n_virt, piece), F32),
            pltpu.VMEM((n_piece, piece, table.shape[1]), BF16),
            pltpu.VMEM((n_chunk, width // LANES, rows, LANES), F32),
            pltpu.VMEM((v_pad // LANES, rows, LANES), F32),
            pltpu.VMEM((n_chunk, width // LANES, rows, LANES), F32),
            pltpu.VMEM((v_pad // LANES, rows, LANES), F32),
            pltpu.VMEM((n_chunk, rows, 2 * width), BF16),
            pltpu.VMEM((n_chunk, rows, 2 * width), BF16),
            pltpu.VMEM(g_shape, F32),
            pltpu.VMEM((n_row,) + g_shape, F32),
            pltpu.SemaphoreType.DMA(((2 + n_chunk) * n_piece,)),
            pltpu.SemaphoreType.DMA((n_chunk + 1,)),
            pltpu.SemaphoreType.DMA((n_chunk + 1,)),
            pltpu.SemaphoreType.DMA((2,)),
            pltpu.SemaphoreType.DMA((2 * n_chunk,)),
        ],
        compiler_params=pltpu.CompilerParams(
            collective_id=0, has_side_effects=True, vmem_limit_bytes=50 * 1024 * 1024
        ),
        name="solve_bins",
    )(downgoing, upgoing, table)
    out_shape = (FREQ_DEV, 2, n_virt, n_local)
    return pl.pallas_call(
        functools.partial(expand_kernel, (n_win, n_chunk, width, n_virt)),
        out_shape=jax.ShapeDtypeStruct(out_shape, F32),
        in_specs=[vmem_spec] * 3,
        out_specs=any_spec,
        scratch_shapes=[pltpu.VMEM(out_shape, F32), pltpu.SemaphoreType.DMA((FREQ_DEV,))],
        compiler_params=pltpu.CompilerParams(vmem_limit_bytes=50 * 1024 * 1024),
        name="expand_bins",
    )(eh, el, y)


def solution(mesh):
    in_specs = (P("win", "row", None), P("win", None, None))
    out_specs = P("win", None, None, "row")
    return jax.shard_map(body, mesh=mesh, in_specs=in_specs, out_specs=out_specs, check_vma=False)
```

```python
import functools
import math

import jax
import jax.numpy as jnp
import numpy as np
from jax import lax
from jax.experimental import pallas as pl
from jax.experimental.pallas import tpu as pltpu
from jax.sharding import PartitionSpec as P

FREQ_DEV = 4
PIECE = 1024
ITERS = 2
DAMPING = 0.5
LANES = 128
MESH = pl.DeviceIdType.MESH
F32, BF16 = jnp.float32, jnp.bfloat16


def dft_table(n_samples, n_bins):
    angles = (np.arange(n_samples)[:, None] * np.arange(1, n_bins + 1)[None, :] % n_samples) * (
        2.0 * math.pi / n_samples
    )
    table = np.stack([np.cos(angles), -np.sin(angles)], axis=2).reshape(n_samples, 2 * n_bins)
    table = (table / math.sqrt(n_samples)).astype(np.float32)
    head = table.astype(BF16)
    tail = (table - head.astype(np.float32)).astype(BF16)
    return np.concatenate([head, tail], axis=1)


def halves(value):
    head = value.astype(BF16)
    return head, (value - head.astype(F32)).astype(BF16)


def dot(first, second, dims):
    return lax.dot_general(first, second, (dims, ((), ())), preferred_element_type=F32)


def accumulate(total, series, table):
    m = series.shape[0]
    head, tail = halves(series)
    part = dot(jnp.concatenate([head, tail], axis=0), table, ((1,), (0,)))
    part = part[:m] + part[m:]
    return part if total is None else total + part


def by_bin(total):
    m = total.shape[0]
    if m % LANES:
        total = jnp.concatenate([total, jnp.zeros((LANES - m % LANES, total.shape[1]), F32)], axis=0)
    total = total.T
    n = total.shape[0] // 2
    return total[:n] + total[n:]


def solve(rhs, gram, n_freq, n_chan, scale):
    rows, n_virt = rhs.shape

    head, tail = halves(gram)
    operator = jnp.concatenate([head, head, tail], axis=1)

    def project(coef):
        c_head, c_tail = halves(coef)
        return dot(operator, jnp.concatenate([c_head, c_tail, c_head], axis=0), ((1,), (0,)))

    def inner(one, two):
        prod = (one * two).reshape(n_freq, rows // n_freq, n_virt)
        total = jnp.sum(prod, axis=1, keepdims=True)
        return jnp.broadcast_to(total, prod.shape).reshape(rows, n_virt)

    filt = jnp.zeros_like(rhs)
    resid, direc = rhs, rhs
    resid_g = project(resid)
    direc_g = resid_g
    norm_old = inner(resid, resid_g)
    for iteration in range(ITERS):
        image = direc_g / n_chan + DAMPING * direc
        curvature = inner(direc_g, image)
        step = norm_old / curvature
        filt = filt + step * direc
        if iteration + 1 < ITERS:
            resid = resid - step * image
            resid_g = resid_g - step * project(image)
            norm_new = inner(resid, resid_g)
            ratio = norm_new / norm_old
            direc = resid + ratio * direc
            direc_g = resid_g + ratio * direc_g
            norm_old = norm_new
    return filt * scale


def solve_kernel(
    dims, x_hbm, up_hbm, tab_hbm, eh_out, el_out, y_out,
    xv, upv, tab, sbuf, ubuf, recv, urecv, eh, el, g_send, g_recv,
    in_sem, send_sem, recv_sem, g_sem, out_sem,
):
    n_win, n_row, n_chunk, width, n_virt, n_chan = dims
    slab = 2 * FREQ_DEV
    rows = n_win * slab
    block = 2 * n_win
    me, row = lax.axis_index("win"), lax.axis_index("row")

    n_piece, piece = tab.shape[0], tab.shape[1]
    loads = []
    for ch in range(n_chunk):
        lines = pl.ds(ch * width, width)
        pairs = []
        for k in range(n_piece):
            span = pl.ds(k * piece, piece)
            if ch == 0:
                pairs.append((tab_hbm.at[span, :], tab.at[k]))
                pairs.append((up_hbm.at[0, :, span], upv.at[k]))
            pairs.append((x_hbm.at[0, lines, span], xv.at[ch, k]))
        loads.append(
            [
                pltpu.make_async_copy(src, dst, in_sem.at[ch, at])
                for at, (src, dst) in enumerate(pairs)
            ]
        )
    for load in loads[0] + loads[min(1, n_chunk - 1)] * (n_chunk > 1):
        load.start()

    win_peers = [lax.rem(me + off, n_win) for off in range(1, n_win)]
    row_peers = [lax.rem(row + off, n_row) for off in range(1, n_row)]
    barrier = pltpu.get_barrier_semaphore()
    for peer in win_peers:
        pl.semaphore_signal(barrier, inc=1, device_id={"win": peer}, device_id_type=MESH)
    for peer in row_peers:
        pl.semaphore_signal(barrier, inc=1, device_id={"row": peer}, device_id_type=MESH)

    def share(src, dst, at):
        own = pl.ds(pl.multiple_of(me * slab, slab), slab)
        dst[:, own, :] = src[:, own, :]
        for peer in win_peers:
            pltpu.make_async_remote_copy(
                src_ref=src.at[:, pl.ds(pl.multiple_of(peer * slab, slab), slab), :],
                dst_ref=dst.at[:, own, :],
                send_sem=send_sem.at[at],
                recv_sem=recv_sem.at[at],
                device_id={"win": peer},
                device_id_type=MESH,
            ).start()

    def put(dst, value):
        for sub in range(dst.shape[0]):
            dst[sub] = value[:, sub * LANES : (sub + 1) * LANES]

    def gather(src, number):
        parts = [src[sub, pl.ds(number, n_win, stride=slab), :] for sub in range(src.shape[0])]
        return jnp.concatenate(parts, axis=1) if len(parts) > 1 else parts[0]

    def await_all(ref, sem):
        part = ref.at[:, pl.ds(0, (n_win - 1) * slab), :]
        pltpu.make_async_copy(part, part, sem).wait()

    for ch in range(n_chunk):
        total = None
        if ch:
            for load in loads[ch]:
                load.wait()
        for k in range(n_piece):
            for load in loads[0][3 * k : 3 * k + 3] if ch == 0 else []:
                load.wait()
            if ch == 0 and k == 0:
                for later in loads[2:]:
                    for load in later:
                        load.start()
            series = xv[ch, k]
            if ch == 0:
                series = jnp.concatenate([series, upv[k]], axis=0)
            total = accumulate(total, series, tab[k])
        put(sbuf.at[ch], by_bin(total[:width]))
        if ch == 0:
            put(ubuf, by_bin(total[width:]))
            pl.semaphore_wait(barrier, n_win + n_row - 2)
        share(sbuf.at[ch], recv.at[ch], ch)
        if ch == 0:
            share(ubuf, urecv, n_chunk)

    gram = None
    stores = []
    for ch in range(n_chunk):
        await_all(recv.at[ch], recv_sem.at[ch])
        left, right = [], []
        for f in range(FREQ_DEV):
            real = gather(recv.at[ch], 2 * f)
            imag = gather(recv.at[ch], 2 * f + 1)
            left += [real, imag]
            right += [-imag, real]
        ext = jnp.concatenate(
            [jnp.concatenate(left, axis=0), jnp.concatenate(right, axis=0)], axis=1
        )
        head, tail = halves(ext)
        eh[ch] = head
        el[ch] = tail
        for number, (src, dst) in enumerate(((eh, eh_out), (el, el_out))):
            store = pltpu.make_async_copy(src.at[ch], dst.at[ch], out_sem.at[2 * ch + number])
            store.start()
            stores.append(store)
        part = dot(
            jnp.concatenate([head, head, tail], axis=1),
            jnp.concatenate([head, tail, head], axis=1),
            ((1,), (1,)),
        )
        gram = part if gram is None else gram + part

    row_id = lax.broadcasted_iota(jnp.int32, (rows, rows), 0) // block
    col_id = lax.broadcasted_iota(jnp.int32, (rows, rows), 1) // block
    same_bin = row_id == col_id
    gram = jnp.where(same_bin, gram, 0.0)
    folded = gram[:block]
    for f in range(1, FREQ_DEV):
        folded = folded + gram[f * block : (f + 1) * block]
    packed = 2 * rows <= LANES
    if packed:
        folded = jnp.concatenate([folded[:n_win], folded[n_win:]], axis=1)
    g_send[...] = folded
    g_recv[row] = folded
    for off, peer in enumerate(row_peers):
        pltpu.make_async_remote_copy(
            src_ref=g_send,
            dst_ref=g_recv.at[row],
            send_sem=g_sem.at[0],
            recv_sem=g_sem.at[1],
            device_id={"row": peer},
            device_id_type=MESH,
        ).start()
    await_all(urecv, recv_sem.at[n_chunk])
    rhs = jnp.concatenate(
        [gather(urecv, number) for number in range(slab)], axis=0
    ) / math.sqrt(n_chan)
    rhs = rhs[:, :n_virt]
    if n_row > 1:
        part = g_recv.at[pl.ds(0, n_row - 1)]
        pltpu.make_async_copy(part, part, g_sem.at[1]).wait()
    folded = g_recv[0]
    for other in range(1, n_row):
        folded = folded + g_recv[other]
    if packed:
        folded = jnp.concatenate([folded[:, :rows], folded[:, rows:]], axis=0)
    gram = jnp.where(same_bin, jnp.concatenate([folded] * FREQ_DEV, axis=0), 0.0)
    y_out[...] = solve(rhs, gram, FREQ_DEV, n_chan, math.sqrt(n_chan / n_win))

    if n_row > 1:
        part = g_recv.at[pl.ds(0, n_row - 1)]
        pltpu.make_async_copy(part, part, g_sem.at[0]).wait()
    for ch in range(n_chunk):
        await_all(recv.at[ch], send_sem.at[ch])
    await_all(urecv, send_sem.at[n_chunk])
    for store in stores:
        store.wait()


def expand_kernel(dims, eh, el, y, out_hbm, ov, sem):
    n_win, n_chunk, width, n_virt = dims
    block = 2 * n_win
    stores = []
    for f in range(FREQ_DEV):
        own = slice(f * block, (f + 1) * block)
        head, tail = halves(y[own, :])
        coef = jnp.concatenate([head, tail, head], axis=0)
        for ch in range(n_chunk):
            big = eh[ch, own, :]
            part = dot(coef, jnp.concatenate([big, big, el[ch, own, :]], axis=0), ((0,), (0,)))
            span = slice(ch * width, (ch + 1) * width)
            ov[f, 0, :, span] = part[:, :width]
            ov[f, 1, :, span] = part[:, width:]
        store = pltpu.make_async_copy(ov.at[f], out_hbm.at[f], sem.at[f])
        store.start()
        stores.append(store)
    for store in stores:
        store.wait()


def body(downgoing, upgoing):
    _, n_local, n_samples = downgoing.shape
    n_virt = upgoing.shape[1]
    n_win, n_row = lax.axis_size("win"), lax.axis_size("row")
    n_chan = n_local * n_row
    width = 256 if n_local % 256 == 0 else 128
    n_chunk = n_local // width
    piece = PIECE if n_samples % PIECE == 0 else n_samples
    n_piece = n_samples // piece
    slab = 2 * FREQ_DEV
    rows = n_win * slab
    block = 2 * n_win
    table = jnp.asarray(dft_table(n_samples, FREQ_DEV * n_win))
    g_shape = (n_win, 2 * rows) if 2 * rows <= LANES else (block, rows)
    v_pad = -(-n_virt // LANES) * LANES
    dims = (n_win, n_row, n_chunk, width, n_virt, n_chan)
    any_spec = pl.BlockSpec(memory_space=pl.ANY)
    vmem_spec = pl.BlockSpec(memory_space=pltpu.VMEM)
    ext = jax.ShapeDtypeStruct((n_chunk, rows, 2 * width), BF16)
    eh, el, y = pl.pallas_call(
        functools.partial(solve_kernel, dims),
        out_shape=(ext, ext, jax.ShapeDtypeStruct((rows, n_virt), F32)),
        in_specs=[pl.BlockSpec(memory_space=pltpu.MemorySpace.HBM)] * 3,
        out_specs=(any_spec, any_spec, vmem_spec),
        scratch_shapes=[
            pltpu.VMEM((n_chunk, n_piece, width, piece), F32),
            pltpu.VMEM((n_piece, n_virt, piece), F32),
            pltpu.VMEM((n_piece, piece, table.shape[1]), BF16),
            pltpu.VMEM((n_chunk, width // LANES, rows, LANES), F32),
            pltpu.VMEM((v_pad // LANES, rows, LANES), F32),
            pltpu.VMEM((n_chunk, width // LANES, rows, LANES), F32),
            pltpu.VMEM((v_pad // LANES, rows, LANES), F32),
            pltpu.VMEM((n_chunk, rows, 2 * width), BF16),
            pltpu.VMEM((n_chunk, rows, 2 * width), BF16),
            pltpu.VMEM(g_shape, F32),
            pltpu.VMEM((n_row,) + g_shape, F32),
            pltpu.SemaphoreType.DMA((n_chunk, 3 * n_piece)),
            pltpu.SemaphoreType.DMA((n_chunk + 1,)),
            pltpu.SemaphoreType.DMA((n_chunk + 1,)),
            pltpu.SemaphoreType.DMA((2,)),
            pltpu.SemaphoreType.DMA((2 * n_chunk,)),
        ],
        compiler_params=pltpu.CompilerParams(
            collective_id=0, has_side_effects=True, vmem_limit_bytes=50 * 1024 * 1024
        ),
        name="solve_bins",
    )(*[pltpu.with_memory_space_constraint(a, pltpu.MemorySpace.HBM) for a in (downgoing, upgoing, table)])
    out_shape = (FREQ_DEV, 2, n_virt, n_local)
    return pl.pallas_call(
        functools.partial(expand_kernel, (n_win, n_chunk, width, n_virt)),
        out_shape=jax.ShapeDtypeStruct(out_shape, F32),
        in_specs=[vmem_spec] * 3,
        out_specs=any_spec,
        scratch_shapes=[pltpu.VMEM(out_shape, F32), pltpu.SemaphoreType.DMA((FREQ_DEV,))],
        compiler_params=pltpu.CompilerParams(vmem_limit_bytes=50 * 1024 * 1024),
        name="expand_bins",
    )(eh, el, y)


def solution(mesh):
    in_specs = (P("win", "row", None), P("win", None, None))
    out_specs = P("win", None, None, "row")
    return jax.shard_map(body, mesh=mesh, in_specs=in_specs, out_specs=out_specs, check_vma=False)
```

```python
import functools
import math

import jax
import jax.numpy as jnp
import numpy as np
from jax import lax
from jax.experimental import pallas as pl
from jax.experimental.pallas import tpu as pltpu
from jax.sharding import PartitionSpec as P

FREQ_DEV = 4
PIECE = 1536
AHEAD = 3
ITERS = 2
DAMPING = 0.5
LANES = 128
MESH = pl.DeviceIdType.MESH
F32, BF16 = jnp.float32, jnp.bfloat16


def dft_table(n_samples, n_bins):
    angles = (np.arange(n_samples)[:, None] * np.arange(1, n_bins + 1)[None, :] % n_samples) * (
        2.0 * math.pi / n_samples
    )
    table = np.stack([np.cos(angles), -np.sin(angles)], axis=2).reshape(n_samples, 2 * n_bins)
    table = (table / math.sqrt(n_samples)).astype(np.float32)
    head = table.astype(BF16)
    tail = (table - head.astype(np.float32)).astype(BF16)
    return np.concatenate([head, tail], axis=1)


def halves(value):
    head = value.astype(BF16)
    return head, (value - head.astype(F32)).astype(BF16)


def dot(first, second, dims):
    return lax.dot_general(first, second, (dims, ((), ())), preferred_element_type=F32)


def split_into(dst, parts):
    total = sum(part.shape[0] for part in parts)
    at = 0
    for part in parts:
        m = part.shape[0]
        head, tail = halves(part[...])
        dst[at : at + m, :] = head
        dst[total + at : total + at + m, :] = tail
        at += m
    return total


def accumulate(total, m, split, table):
    part = dot(split[: 2 * m, :], table, ((1,), (0,)))
    part = part[:m] + part[m:]
    return part if total is None else total + part


def by_bin(total):
    m = total.shape[0]
    if m % LANES:
        total = jnp.concatenate([total, jnp.zeros((LANES - m % LANES, total.shape[1]), F32)], axis=0)
    total = total.T
    n = total.shape[0] // 2
    return total[:n] + total[n:]


def solve(rhs, gram, n_freq, n_chan, scale):
    rows, n_virt = rhs.shape

    head, tail = halves(gram)
    operator = jnp.concatenate([head, head, tail], axis=1)

    def project(coef):
        c_head, c_tail = halves(coef)
        return dot(operator, jnp.concatenate([c_head, c_tail, c_head], axis=0), ((1,), (0,)))

    def inner(one, two):
        prod = (one * two).reshape(n_freq, rows // n_freq, n_virt)
        total = jnp.sum(prod, axis=1, keepdims=True)
        return jnp.broadcast_to(total, prod.shape).reshape(rows, n_virt)

    filt = jnp.zeros_like(rhs)
    resid, direc = rhs, rhs
    resid_g = project(resid)
    direc_g = resid_g
    norm_old = inner(resid, resid_g)
    for iteration in range(ITERS):
        image = direc_g / n_chan + DAMPING * direc
        curvature = inner(direc_g, image)
        step = norm_old / curvature
        filt = filt + step * direc
        if iteration + 1 < ITERS:
            resid = resid - step * image
            resid_g = resid_g - step * project(image)
            norm_new = inner(resid, resid_g)
            ratio = norm_new / norm_old
            direc = resid + ratio * direc
            direc_g = resid_g + ratio * direc_g
            norm_old = norm_new
    return filt * scale


def solve_kernel(
    dims, x_hbm, up_hbm, tab_hbm, eh_out, el_out, y_out,
    xv, upv, tab, split_a, split_b, sbuf, ubuf, recv, urecv, eh, el, g_send, g_recv,
    in_sem, send_sem, recv_sem, g_sem, out_sem,
):
    n_win, n_row, n_chunk, width, n_virt, n_chan = dims
    slab = 2 * FREQ_DEV
    rows = n_win * slab
    block = 2 * n_win
    me, row = lax.axis_index("win"), lax.axis_index("row")

    n_piece, piece = tab.shape[0], tab.shape[1]
    pair = (split_a, split_b)
    n_piece, piece = tab.shape[0], tab.shape[1]
    pair = (split_a, split_b)
    order = [(ch, k) for ch in range(n_chunk) for k in range(n_piece)]
    loads = []
    for ch, k in order:
        span = pl.ds(k * piece, piece)
        pairs = [(x_hbm.at[0, pl.ds(ch * width, width), span], xv.at[ch, k])]
        if ch == 0:
            pairs = [(tab_hbm.at[span, :], tab.at[k])] + pairs + [(up_hbm.at[0, :, span], upv.at[k])]
        loads.append(
            [
                pltpu.make_async_copy(src, dst, in_sem.at[len(loads), at])
                for at, (src, dst) in enumerate(pairs)
            ]
        )

    def start(number):
        for load in loads[number] if number < len(loads) else []:
            load.start()

    def split(number):
        for load in loads[number]:
            load.wait()
        start(number + AHEAD)
        ch, k = order[number]
        parts = [xv.at[ch, k]] + ([upv.at[k]] if ch == 0 else [])
        return split_into(pair[number % 2], parts)

    for number in range(AHEAD):
        start(number)

    win_peers = [lax.rem(me + off, n_win) for off in range(1, n_win)]
    row_peers = [lax.rem(row + off, n_row) for off in range(1, n_row)]
    barrier = pltpu.get_barrier_semaphore()
    for peer in win_peers:
        pl.semaphore_signal(barrier, inc=1, device_id={"win": peer}, device_id_type=MESH)
    for peer in row_peers:
        pl.semaphore_signal(barrier, inc=1, device_id={"row": peer}, device_id_type=MESH)

    def share(src, dst, at):
        own = pl.ds(pl.multiple_of(me * slab, slab), slab)
        dst[:, own, :] = src[:, own, :]
        for peer in win_peers:
            pltpu.make_async_remote_copy(
                src_ref=src.at[:, pl.ds(pl.multiple_of(peer * slab, slab), slab), :],
                dst_ref=dst.at[:, own, :],
                send_sem=send_sem.at[at],
                recv_sem=recv_sem.at[at],
                device_id={"win": peer},
                device_id_type=MESH,
            ).start()

    def put(dst, value):
        for sub in range(dst.shape[0]):
            dst[sub] = value[:, sub * LANES : (sub + 1) * LANES]

    def gather(src, number):
        parts = [src[sub, pl.ds(number, n_win, stride=slab), :] for sub in range(src.shape[0])]
        return jnp.concatenate(parts, axis=1) if len(parts) > 1 else parts[0]

    def await_all(ref, sem):
        part = ref.at[:, pl.ds(0, (n_win - 1) * slab), :]
        pltpu.make_async_copy(part, part, sem).wait()

    lines = split(0)
    total = None
    for number, (ch, k) in enumerate(order):
        later = split(number + 1) if number + 1 < len(order) else None
        total = accumulate(total, lines, pair[number % 2], tab[k])
        lines = later
        if k + 1 < n_piece:
            continue
        put(sbuf.at[ch], by_bin(total[:width]))
        if ch == 0:
            put(ubuf, by_bin(total[width:]))
            pl.semaphore_wait(barrier, n_win + n_row - 2)
        share(sbuf.at[ch], recv.at[ch], ch)
        if ch == 0:
            share(ubuf, urecv, n_chunk)
        total = None

    gram = None
    stores = []
    for ch in range(n_chunk):
        await_all(recv.at[ch], recv_sem.at[ch])
        left, right = [], []
        for f in range(FREQ_DEV):
            real = gather(recv.at[ch], 2 * f)
            imag = gather(recv.at[ch], 2 * f + 1)
            left += [real, imag]
            right += [-imag, real]
        ext = jnp.concatenate(
            [jnp.concatenate(left, axis=0), jnp.concatenate(right, axis=0)], axis=1
        )
        head, tail = halves(ext)
        eh[ch] = head
        el[ch] = tail
        for number, (src, dst) in enumerate(((eh, eh_out), (el, el_out))):
            store = pltpu.make_async_copy(src.at[ch], dst.at[ch], out_sem.at[2 * ch + number])
            store.start()
            stores.append(store)
        part = dot(
            jnp.concatenate([head, head, tail], axis=1),
            jnp.concatenate([head, tail, head], axis=1),
            ((1,), (1,)),
        )
        gram = part if gram is None else gram + part

    row_id = lax.broadcasted_iota(jnp.int32, (rows, rows), 0) // block
    col_id = lax.broadcasted_iota(jnp.int32, (rows, rows), 1) // block
    same_bin = row_id == col_id
    gram = jnp.where(same_bin, gram, 0.0)
    folded = gram[:block]
    for f in range(1, FREQ_DEV):
        folded = folded + gram[f * block : (f + 1) * block]
    packed = 2 * rows <= LANES
    if packed:
        folded = jnp.concatenate([folded[:n_win], folded[n_win:]], axis=1)
    g_send[...] = folded
    g_recv[row] = folded
    for off, peer in enumerate(row_peers):
        pltpu.make_async_remote_copy(
            src_ref=g_send,
            dst_ref=g_recv.at[row],
            send_sem=g_sem.at[0],
            recv_sem=g_sem.at[1],
            device_id={"row": peer},
            device_id_type=MESH,
        ).start()
    await_all(urecv, recv_sem.at[n_chunk])
    rhs = jnp.concatenate(
        [gather(urecv, number) for number in range(slab)], axis=0
    ) / math.sqrt(n_chan)
    rhs = rhs[:, :n_virt]
    if n_row > 1:
        part = g_recv.at[pl.ds(0, n_row - 1)]
        pltpu.make_async_copy(part, part, g_sem.at[1]).wait()
    folded = g_recv[0]
    for other in range(1, n_row):
        folded = folded + g_recv[other]
    if packed:
        folded = jnp.concatenate([folded[:, :rows], folded[:, rows:]], axis=0)
    gram = jnp.where(same_bin, jnp.concatenate([folded] * FREQ_DEV, axis=0), 0.0)
    y_out[...] = solve(rhs, gram, FREQ_DEV, n_chan, math.sqrt(n_chan / n_win))

    if n_row > 1:
        part = g_recv.at[pl.ds(0, n_row - 1)]
        pltpu.make_async_copy(part, part, g_sem.at[0]).wait()
    for ch in range(n_chunk):
        await_all(recv.at[ch], send_sem.at[ch])
    await_all(urecv, send_sem.at[n_chunk])
    for store in stores:
        store.wait()


def expand_kernel(dims, eh, el, y, out_hbm, ov, sem):
    n_win, n_chunk, width, n_virt = dims
    block = 2 * n_win
    stores = []
    for f in range(FREQ_DEV):
        own = slice(f * block, (f + 1) * block)
        head, tail = halves(y[own, :])
        coef = jnp.concatenate([head, tail, head], axis=0)
        for ch in range(n_chunk):
            big = eh[ch, own, :]
            part = dot(coef, jnp.concatenate([big, big, el[ch, own, :]], axis=0), ((0,), (0,)))
            span = slice(ch * width, (ch + 1) * width)
            ov[f, 0, :, span] = part[:, :width]
            ov[f, 1, :, span] = part[:, width:]
        store = pltpu.make_async_copy(ov.at[f], out_hbm.at[f], sem.at[f])
        store.start()
        stores.append(store)
    for store in stores:
        store.wait()


def body(downgoing, upgoing):
    _, n_local, n_samples = downgoing.shape
    n_virt = upgoing.shape[1]
    n_win, n_row = lax.axis_size("win"), lax.axis_size("row")
    n_chan = n_local * n_row
    width = 256 if n_local % 256 == 0 else 128
    n_chunk = n_local // width
    piece = PIECE if n_samples % PIECE == 0 else n_samples
    n_piece = n_samples // piece
    slab = 2 * FREQ_DEV
    rows = n_win * slab
    block = 2 * n_win
    table = jnp.asarray(dft_table(n_samples, FREQ_DEV * n_win))
    g_shape = (n_win, 2 * rows) if 2 * rows <= LANES else (block, rows)
    v_pad = -(-n_virt // LANES) * LANES
    dims = (n_win, n_row, n_chunk, width, n_virt, n_chan)
    any_spec = pl.BlockSpec(memory_space=pl.ANY)
    vmem_spec = pl.BlockSpec(memory_space=pltpu.VMEM)
    ext = jax.ShapeDtypeStruct((n_chunk, rows, 2 * width), BF16)
    eh, el, y = pl.pallas_call(
        functools.partial(solve_kernel, dims),
        out_shape=(ext, ext, jax.ShapeDtypeStruct((rows, n_virt), F32)),
        in_specs=[pl.BlockSpec(memory_space=pltpu.MemorySpace.HBM)] * 3,
        out_specs=(any_spec, any_spec, vmem_spec),
        scratch_shapes=[
            pltpu.VMEM((n_chunk, n_piece, width, piece), F32),
            pltpu.VMEM((n_piece, n_virt, piece), F32),
            pltpu.VMEM((n_piece, piece, table.shape[1]), BF16),
            pltpu.VMEM((2 * (width + n_virt), piece), BF16),
            pltpu.VMEM((2 * (width + n_virt), piece), BF16),
            pltpu.VMEM((n_chunk, width // LANES, rows, LANES), F32),
            pltpu.VMEM((v_pad // LANES, rows, LANES), F32),
            pltpu.VMEM((n_chunk, width // LANES, rows, LANES), F32),
            pltpu.VMEM((v_pad // LANES, rows, LANES), F32),
            pltpu.VMEM((n_chunk, rows, 2 * width), BF16),
            pltpu.VMEM((n_chunk, rows, 2 * width), BF16),
            pltpu.VMEM(g_shape, F32),
            pltpu.VMEM((n_row,) + g_shape, F32),
            pltpu.SemaphoreType.DMA((n_chunk * n_piece, 3)),
            pltpu.SemaphoreType.DMA((n_chunk + 1,)),
            pltpu.SemaphoreType.DMA((n_chunk + 1,)),
            pltpu.SemaphoreType.DMA((2,)),
            pltpu.SemaphoreType.DMA((2 * n_chunk,)),
        ],
        compiler_params=pltpu.CompilerParams(
            collective_id=0, has_side_effects=True, vmem_limit_bytes=50 * 1024 * 1024
        ),
        name="solve_bins",
    )(*[pltpu.with_memory_space_constraint(a, pltpu.MemorySpace.HBM) for a in (downgoing, upgoing, table)])
    out_shape = (FREQ_DEV, 2, n_virt, n_local)
    return pl.pallas_call(
        functools.partial(expand_kernel, (n_win, n_chunk, width, n_virt)),
        out_shape=jax.ShapeDtypeStruct(out_shape, F32),
        in_specs=[vmem_spec] * 3,
        out_specs=any_spec,
        scratch_shapes=[pltpu.VMEM(out_shape, F32), pltpu.SemaphoreType.DMA((FREQ_DEV,))],
        compiler_params=pltpu.CompilerParams(vmem_limit_bytes=50 * 1024 * 1024),
        name="expand_bins",
    )(eh, el, y)


def solution(mesh):
    in_specs = (P("win", "row", None), P("win", None, None))
    out_specs = P("win", None, None, "row")
    return jax.shard_map(body, mesh=mesh, in_specs=in_specs, out_specs=out_specs, check_vma=False)
```

```python
import functools
import math

import jax
import jax.numpy as jnp
import numpy as np
from jax import lax
from jax.experimental import pallas as pl
from jax.experimental.pallas import tpu as pltpu
from jax.sharding import PartitionSpec as P

FREQ_DEV = 4
PIECE = 1024
STEP = 256
ITERS = 2
DAMPING = 0.5
LANES = 128
MESH = pl.DeviceIdType.MESH
F32, BF16 = jnp.float32, jnp.bfloat16


def dft_table(n_samples, n_bins):
    angles = (np.arange(n_samples)[:, None] * np.arange(1, n_bins + 1)[None, :] % n_samples) * (
        2.0 * math.pi / n_samples
    )
    table = np.stack([np.cos(angles), -np.sin(angles)], axis=2).reshape(n_samples, 2 * n_bins)
    table = (table / math.sqrt(n_samples)).astype(np.float32)
    head = table.astype(BF16)
    tail = (table - head.astype(np.float32)).astype(BF16)
    return np.concatenate([head, tail], axis=1)


def halves(value):
    head = value.astype(BF16)
    return head, (value - head.astype(F32)).astype(BF16)


def dot(first, second, dims):
    return lax.dot_general(first, second, (dims, ((), ())), preferred_element_type=F32)


def accumulate(total, parts, table):
    for at in range(0, table.shape[0], STEP):
        span = slice(at, at + STEP)
        series = [part[:, span] for part in parts]
        series = jnp.concatenate(series, axis=0) if len(series) > 1 else series[0]
        m = series.shape[0]
        head, tail = halves(series)
        weights = table[span, :]
        part = dot(head, weights, ((1,), (0,))) + dot(tail, weights, ((1,), (0,)))
        total = part if total is None else total + part
    return total


def by_bin(total):
    m = total.shape[0]
    if m % LANES:
        total = jnp.concatenate([total, jnp.zeros((LANES - m % LANES, total.shape[1]), F32)], axis=0)
    total = total.T
    n = total.shape[0] // 2
    return total[:n] + total[n:]


def solve(rhs, gram, n_freq, n_chan, scale):
    rows, n_virt = rhs.shape

    head, tail = halves(gram)
    operator = jnp.concatenate([head, head, tail], axis=1)

    def project(coef):
        c_head, c_tail = halves(coef)
        return dot(operator, jnp.concatenate([c_head, c_tail, c_head], axis=0), ((1,), (0,)))

    def inner(one, two):
        prod = (one * two).reshape(n_freq, rows // n_freq, n_virt)
        total = jnp.sum(prod, axis=1, keepdims=True)
        return jnp.broadcast_to(total, prod.shape).reshape(rows, n_virt)

    filt = jnp.zeros_like(rhs)
    resid, direc = rhs, rhs
    resid_g = project(resid)
    direc_g = resid_g
    norm_old = inner(resid, resid_g)
    for iteration in range(ITERS):
        image = direc_g / n_chan + DAMPING * direc
        curvature = inner(direc_g, image)
        step = norm_old / curvature
        filt = filt + step * direc
        if iteration + 1 < ITERS:
            resid = resid - step * image
            resid_g = resid_g - step * project(image)
            norm_new = inner(resid, resid_g)
            ratio = norm_new / norm_old
            direc = resid + ratio * direc
            direc_g = resid_g + ratio * direc_g
            norm_old = norm_new
    return filt * scale


def solve_kernel(
    dims, x_hbm, up_hbm, tab_hbm, eh_out, el_out, y_out,
    xv, upv, tab, sbuf, ubuf, recv, urecv, eh, el, g_send, g_recv,
    in_sem, send_sem, recv_sem, g_sem, out_sem,
):
    n_win, n_row, n_chunk, width, n_virt, n_chan = dims
    slab = 2 * FREQ_DEV
    rows = n_win * slab
    block = 2 * n_win
    me, row = lax.axis_index("win"), lax.axis_index("row")

    n_piece, piece = tab.shape[0], tab.shape[1]
    loads = []
    for ch in range(n_chunk):
        lines = pl.ds(ch * width, width)
        pairs = []
        for k in range(n_piece):
            span = pl.ds(k * piece, piece)
            if ch == 0:
                pairs.append((tab_hbm.at[span, :], tab.at[k]))
                pairs.append((up_hbm.at[0, :, span], upv.at[k]))
            pairs.append((x_hbm.at[0, lines, span], xv.at[ch, k]))
        loads.append(
            [
                pltpu.make_async_copy(src, dst, in_sem.at[ch, at])
                for at, (src, dst) in enumerate(pairs)
            ]
        )
    for load in loads[0] + loads[min(1, n_chunk - 1)] * (n_chunk > 1):
        load.start()

    win_peers = [lax.rem(me + off, n_win) for off in range(1, n_win)]
    row_peers = [lax.rem(row + off, n_row) for off in range(1, n_row)]
    barrier = pltpu.get_barrier_semaphore()
    for peer in win_peers:
        pl.semaphore_signal(barrier, inc=1, device_id={"win": peer}, device_id_type=MESH)
    for peer in row_peers:
        pl.semaphore_signal(barrier, inc=1, device_id={"row": peer}, device_id_type=MESH)

    def share(src, dst, at):
        own = pl.ds(pl.multiple_of(me * slab, slab), slab)
        dst[:, own, :] = src[:, own, :]
        for peer in win_peers:
            pltpu.make_async_remote_copy(
                src_ref=src.at[:, pl.ds(pl.multiple_of(peer * slab, slab), slab), :],
                dst_ref=dst.at[:, own, :],
                send_sem=send_sem.at[at],
                recv_sem=recv_sem.at[at],
                device_id={"win": peer},
                device_id_type=MESH,
            ).start()

    def put(dst, value):
        for sub in range(dst.shape[0]):
            dst[sub] = value[:, sub * LANES : (sub + 1) * LANES]

    def gather(src, number):
        parts = [src[sub, pl.ds(number, n_win, stride=slab), :] for sub in range(src.shape[0])]
        return jnp.concatenate(parts, axis=1) if len(parts) > 1 else parts[0]

    def await_all(ref, sem):
        part = ref.at[:, pl.ds(0, (n_win - 1) * slab), :]
        pltpu.make_async_copy(part, part, sem).wait()

    for ch in range(n_chunk):
        total = None
        if ch:
            for load in loads[ch]:
                load.wait()
        for k in range(n_piece):
            for load in loads[0][3 * k : 3 * k + 3] if ch == 0 else []:
                load.wait()
            if ch == 0 and k == 0:
                for later in loads[2:]:
                    for load in later:
                        load.start()
            parts = [xv.at[ch, k]] + ([upv.at[k]] if ch == 0 else [])
            total = accumulate(total, parts, tab.at[k])
        put(sbuf.at[ch], by_bin(total[:width]))
        if ch == 0:
            put(ubuf, by_bin(total[width:]))
            pl.semaphore_wait(barrier, n_win + n_row - 2)
        share(sbuf.at[ch], recv.at[ch], ch)
        if ch == 0:
            share(ubuf, urecv, n_chunk)

    gram = None
    stores = []
    for ch in range(n_chunk):
        await_all(recv.at[ch], recv_sem.at[ch])
        left, right = [], []
        for f in range(FREQ_DEV):
            real = gather(recv.at[ch], 2 * f)
            imag = gather(recv.at[ch], 2 * f + 1)
            left += [real, imag]
            right += [-imag, real]
        ext = jnp.concatenate(
            [jnp.concatenate(left, axis=0), jnp.concatenate(right, axis=0)], axis=1
        )
        head, tail = halves(ext)
        eh[ch] = head
        el[ch] = tail
        for number, (src, dst) in enumerate(((eh, eh_out), (el, el_out))):
            store = pltpu.make_async_copy(src.at[ch], dst.at[ch], out_sem.at[2 * ch + number])
            store.start()
            stores.append(store)
        part = dot(
            jnp.concatenate([head, head, tail], axis=1),
            jnp.concatenate([head, tail, head], axis=1),
            ((1,), (1,)),
        )
        gram = part if gram is None else gram + part

    row_id = lax.broadcasted_iota(jnp.int32, (rows, rows), 0) // block
    col_id = lax.broadcasted_iota(jnp.int32, (rows, rows), 1) // block
    same_bin = row_id == col_id
    gram = jnp.where(same_bin, gram, 0.0)
    folded = gram[:block]
    for f in range(1, FREQ_DEV):
        folded = folded + gram[f * block : (f + 1) * block]
    packed = 2 * rows <= LANES
    if packed:
        folded = jnp.concatenate([folded[:n_win], folded[n_win:]], axis=1)
    g_send[...] = folded
    g_recv[row] = folded
    for off, peer in enumerate(row_peers):
        pltpu.make_async_remote_copy(
            src_ref=g_send,
            dst_ref=g_recv.at[row],
            send_sem=g_sem.at[0],
            recv_sem=g_sem.at[1],
            device_id={"row": peer},
            device_id_type=MESH,
        ).start()
    await_all(urecv, recv_sem.at[n_chunk])
    rhs = jnp.concatenate(
        [gather(urecv, number) for number in range(slab)], axis=0
    ) / math.sqrt(n_chan)
    rhs = rhs[:, :n_virt]
    if n_row > 1:
        part = g_recv.at[pl.ds(0, n_row - 1)]
        pltpu.make_async_copy(part, part, g_sem.at[1]).wait()
    folded = g_recv[0]
    for other in range(1, n_row):
        folded = folded + g_recv[other]
    if packed:
        folded = jnp.concatenate([folded[:, :rows], folded[:, rows:]], axis=0)
    gram = jnp.where(same_bin, jnp.concatenate([folded] * FREQ_DEV, axis=0), 0.0)
    y_out[...] = solve(rhs, gram, FREQ_DEV, n_chan, math.sqrt(n_chan / n_win))

    if n_row > 1:
        part = g_recv.at[pl.ds(0, n_row - 1)]
        pltpu.make_async_copy(part, part, g_sem.at[0]).wait()
    for ch in range(n_chunk):
        await_all(recv.at[ch], send_sem.at[ch])
    await_all(urecv, send_sem.at[n_chunk])
    for store in stores:
        store.wait()


def expand_kernel(dims, eh, el, y, out_hbm, ov, sem):
    n_win, n_chunk, width, n_virt = dims
    block = 2 * n_win
    rows = FREQ_DEV * block
    row_id = lax.broadcasted_iota(jnp.int32, (rows, FREQ_DEV * n_virt), 0) // block
    col_id = lax.broadcasted_iota(jnp.int32, (rows, FREQ_DEV * n_virt), 1) // n_virt
    coef = jnp.where(row_id == col_id, jnp.concatenate([y[...]] * FREQ_DEV, axis=1), 0.0).T
    head, tail = halves(coef)
    coef = jnp.concatenate([head, tail, head], axis=1)
    stores = []
    for ch in range(n_chunk):
        big = eh[ch]
        part = dot(coef, jnp.concatenate([big, big, el[ch]], axis=0), ((1,), (0,)))
        span = slice(ch * width, (ch + 1) * width)
        for f in range(FREQ_DEV):
            own = slice(f * n_virt, (f + 1) * n_virt)
            ov[f, 0, :, span] = part[own, :width]
            ov[f, 1, :, span] = part[own, width:]
        lanes = pl.ds(ch * width, width)
        store = pltpu.make_async_copy(ov.at[:, :, :, lanes], out_hbm.at[:, :, :, lanes], sem.at[ch])
        store.start()
        stores.append(store)
    for store in stores:
        store.wait()


def body(downgoing, upgoing):
    _, n_local, n_samples = downgoing.shape
    n_virt = upgoing.shape[1]
    n_win, n_row = lax.axis_size("win"), lax.axis_size("row")
    n_chan = n_local * n_row
    width = 256 if n_local % 256 == 0 else 128
    n_chunk = n_local // width
    piece = PIECE if n_samples % PIECE == 0 else n_samples
    n_piece = n_samples // piece
    slab = 2 * FREQ_DEV
    rows = n_win * slab
    block = 2 * n_win
    table = jnp.asarray(dft_table(n_samples, FREQ_DEV * n_win))
    g_shape = (n_win, 2 * rows) if 2 * rows <= LANES else (block, rows)
    v_pad = -(-n_virt // LANES) * LANES
    dims = (n_win, n_row, n_chunk, width, n_virt, n_chan)
    any_spec = pl.BlockSpec(memory_space=pl.ANY)
    vmem_spec = pl.BlockSpec(memory_space=pltpu.VMEM)
    ext = jax.ShapeDtypeStruct((n_chunk, rows, 2 * width), BF16)
    eh, el, y = pl.pallas_call(
        functools.partial(solve_kernel, dims),
        out_shape=(ext, ext, jax.ShapeDtypeStruct((rows, n_virt), F32)),
        in_specs=[pl.BlockSpec(memory_space=pltpu.MemorySpace.HBM)] * 3,
        out_specs=(any_spec, any_spec, vmem_spec),
        scratch_shapes=[
            pltpu.VMEM((n_chunk, n_piece, width, piece), F32),
            pltpu.VMEM((n_piece, n_virt, piece), F32),
            pltpu.VMEM((n_piece, piece, table.shape[1]), BF16),
            pltpu.VMEM((n_chunk, width // LANES, rows, LANES), F32),
            pltpu.VMEM((v_pad // LANES, rows, LANES), F32),
            pltpu.VMEM((n_chunk, width // LANES, rows, LANES), F32),
            pltpu.VMEM((v_pad // LANES, rows, LANES), F32),
            pltpu.VMEM((n_chunk, rows, 2 * width), BF16),
            pltpu.VMEM((n_chunk, rows, 2 * width), BF16),
            pltpu.VMEM(g_shape, F32),
            pltpu.VMEM((n_row,) + g_shape, F32),
            pltpu.SemaphoreType.DMA((n_chunk, 3 * n_piece)),
            pltpu.SemaphoreType.DMA((n_chunk + 1,)),
            pltpu.SemaphoreType.DMA((n_chunk + 1,)),
            pltpu.SemaphoreType.DMA((2,)),
            pltpu.SemaphoreType.DMA((2 * n_chunk,)),
        ],
        compiler_params=pltpu.CompilerParams(
            collective_id=0, has_side_effects=True, vmem_limit_bytes=50 * 1024 * 1024
        ),
        name="solve_bins",
    )(*[pltpu.with_memory_space_constraint(a, pltpu.MemorySpace.HBM) for a in (downgoing, upgoing, table)])
    out_shape = (FREQ_DEV, 2, n_virt, n_local)
    return pl.pallas_call(
        functools.partial(expand_kernel, (n_win, n_chunk, width, n_virt)),
        out_shape=jax.ShapeDtypeStruct(out_shape, F32),
        in_specs=[vmem_spec] * 3,
        out_specs=any_spec,
        scratch_shapes=[pltpu.VMEM(out_shape, F32), pltpu.SemaphoreType.DMA((n_chunk,))],
        compiler_params=pltpu.CompilerParams(vmem_limit_bytes=50 * 1024 * 1024),
        name="expand_bins",
    )(eh, el, y)


def solution(mesh):
    in_specs = (P("win", "row", None), P("win", None, None))
    out_specs = P("win", None, None, "row")
    return jax.shard_map(body, mesh=mesh, in_specs=in_specs, out_specs=out_specs, check_vma=False)
```

```python
import functools
import math

import jax
import jax.numpy as jnp
import numpy as np
from jax import lax
from jax.experimental import pallas as pl
from jax.experimental.pallas import tpu as pltpu
from jax.sharding import PartitionSpec as P

FREQ_DEV = 4
PIECE = 1024
STEP = 256
ITERS = 2
DAMPING = 0.5
LANES = 128
MESH = pl.DeviceIdType.MESH
F32, BF16 = jnp.float32, jnp.bfloat16


def dft_table(n_samples, n_bins):
    angles = (np.arange(n_samples)[:, None] * np.arange(1, n_bins + 1)[None, :] % n_samples) * (
        2.0 * math.pi / n_samples
    )
    table = np.stack([np.cos(angles), -np.sin(angles)], axis=2).reshape(n_samples, 2 * n_bins)
    table = (table / math.sqrt(n_samples)).astype(np.float32)
    head = table.astype(BF16)
    tail = (table - head.astype(np.float32)).astype(BF16)
    return np.concatenate([head, tail], axis=1)


def halves(value):
    head = value.astype(BF16)
    return head, (value - head.astype(F32)).astype(BF16)


def dot(first, second, dims):
    return lax.dot_general(first, second, (dims, ((), ())), preferred_element_type=F32)


def accumulate(total, parts, table):
    for at in range(0, table.shape[0], STEP):
        span = slice(at, at + STEP)
        series = [part[:, span] for part in parts]
        series = jnp.concatenate(series, axis=0) if len(series) > 1 else series[0]
        m = series.shape[0]
        head, tail = halves(series)
        weights = table[span, :]
        part = dot(head, weights, ((1,), (0,))) + dot(tail, weights, ((1,), (0,)))
        total = part if total is None else total + part
    return total


def by_bin(total):
    m = total.shape[0]
    if m % LANES:
        total = jnp.concatenate([total, jnp.zeros((LANES - m % LANES, total.shape[1]), F32)], axis=0)
    total = total.T
    n = total.shape[0] // 2
    return total[:n] + total[n:]


def solve(rhs, gram, n_freq, n_chan, scale):
    rows, n_virt = rhs.shape

    head, tail = halves(gram)
    operator = jnp.concatenate([head, head, tail], axis=1)

    def project(coef):
        c_head, c_tail = halves(coef)
        return dot(operator, jnp.concatenate([c_head, c_tail, c_head], axis=0), ((1,), (0,)))

    def inner(one, two):
        prod = (one * two).reshape(n_freq, rows // n_freq, n_virt)
        total = jnp.sum(prod, axis=1, keepdims=True)
        return jnp.broadcast_to(total, prod.shape).reshape(rows, n_virt)

    filt = jnp.zeros_like(rhs)
    resid, direc = rhs, rhs
    resid_g = project(resid)
    direc_g = resid_g
    norm_old = inner(resid, resid_g)
    for iteration in range(ITERS):
        image = direc_g / n_chan + DAMPING * direc
        curvature = inner(direc_g, image)
        step = norm_old / curvature
        filt = filt + step * direc
        if iteration + 1 < ITERS:
            resid = resid - step * image
            resid_g = resid_g - step * project(image)
            norm_new = inner(resid, resid_g)
            ratio = norm_new / norm_old
            direc = resid + ratio * direc
            direc_g = resid_g + ratio * direc_g
            norm_old = norm_new
    return filt * scale


def solve_kernel(
    dims, x_hbm, up_hbm, tab_hbm, eh_out, el_out, y_out,
    xv, upv, tab, sbuf, recv, eh, el, g_send, g_recv,
    in_sem, send_sem, recv_sem, g_sem, out_sem,
):
    n_win, n_row, n_chunk, width, n_virt, n_chan = dims
    slab = 2 * FREQ_DEV
    rows = n_win * slab
    block = 2 * n_win
    me, row = lax.axis_index("win"), lax.axis_index("row")

    n_piece, piece = tab.shape[0], tab.shape[1]
    loads = []
    for ch in range(n_chunk):
        lines = pl.ds(ch * width, width)
        pairs = []
        for k in range(n_piece):
            span = pl.ds(k * piece, piece)
            if ch == 0:
                pairs.append((tab_hbm.at[span, :], tab.at[k]))
                pairs.append((up_hbm.at[0, :, span], upv.at[k]))
            pairs.append((x_hbm.at[0, lines, span], xv.at[ch, k]))
        loads.append(
            [
                pltpu.make_async_copy(src, dst, in_sem.at[ch, at])
                for at, (src, dst) in enumerate(pairs)
            ]
        )
    for load in loads[0]:
        load.start()

    win_peers = [lax.rem(me + off, n_win) for off in range(1, n_win)]
    row_peers = [lax.rem(row + off, n_row) for off in range(1, n_row)]
    barrier = pltpu.get_barrier_semaphore()
    for peer in win_peers:
        pl.semaphore_signal(barrier, inc=1, device_id={"win": peer}, device_id_type=MESH)
    for peer in row_peers:
        pl.semaphore_signal(barrier, inc=1, device_id={"row": peer}, device_id_type=MESH)

    n_sub = width // LANES

    def slabs(buf, ch):
        return buf.at[ch, pl.ds(0, buf.shape[1] if ch == 0 else n_sub)]

    def share(src, dst, at):
        own = pl.ds(pl.multiple_of(me * slab, slab), slab)
        dst[:, own, :] = src[:, own, :]
        for peer in win_peers:
            pltpu.make_async_remote_copy(
                src_ref=src.at[:, pl.ds(pl.multiple_of(peer * slab, slab), slab), :],
                dst_ref=dst.at[:, own, :],
                send_sem=send_sem.at[at],
                recv_sem=recv_sem.at[at],
                device_id={"win": peer},
                device_id_type=MESH,
            ).start()

    def put(dst, value):
        for sub in range(value.shape[1] // LANES):
            dst[sub] = value[:, sub * LANES : (sub + 1) * LANES]

    def gather(src, number, subs):
        parts = [src[sub, pl.ds(number, n_win, stride=slab), :] for sub in subs]
        return jnp.concatenate(parts, axis=1) if len(parts) > 1 else parts[0]

    def await_all(ref, sem):
        part = ref.at[:, pl.ds(0, (n_win - 1) * slab), :]
        pltpu.make_async_copy(part, part, sem).wait()

    for ch in range(n_chunk):
        total = None
        if ch:
            for load in loads[ch]:
                load.wait()
        for k in range(n_piece):
            for load in loads[0][3 * k : 3 * k + 3] if ch == 0 else []:
                load.wait()
            if ch == 0:
                until = k + 2 if k + 1 < n_piece else n_chunk
                for later in loads[k + 1 : until]:
                    for load in later:
                        load.start()
            parts = [xv.at[ch, k]] + ([upv.at[k]] if ch == 0 else [])
            total = accumulate(total, parts, tab.at[k])
        put(sbuf.at[ch], by_bin(total))
        if ch == 0:
            pl.semaphore_wait(barrier, n_win + n_row - 2)
        share(slabs(sbuf, ch), slabs(recv, ch), ch)

    gram = None
    stores = []
    for ch in range(n_chunk):
        await_all(slabs(recv, ch), recv_sem.at[ch])
        left, right = [], []
        for f in range(FREQ_DEV):
            real = gather(recv.at[ch], 2 * f, range(n_sub))
            imag = gather(recv.at[ch], 2 * f + 1, range(n_sub))
            left += [real, imag]
            right += [-imag, real]
        ext = jnp.concatenate(
            [jnp.concatenate(left, axis=0), jnp.concatenate(right, axis=0)], axis=1
        )
        head, tail = halves(ext)
        eh[ch] = head
        el[ch] = tail
        for number, (src, dst) in enumerate(((eh, eh_out), (el, el_out))):
            store = pltpu.make_async_copy(src.at[ch], dst.at[ch], out_sem.at[2 * ch + number])
            store.start()
            stores.append(store)
        part = dot(
            jnp.concatenate([head, head, tail], axis=1),
            jnp.concatenate([head, tail, head], axis=1),
            ((1,), (1,)),
        )
        gram = part if gram is None else gram + part

    row_id = lax.broadcasted_iota(jnp.int32, (rows, rows), 0) // block
    col_id = lax.broadcasted_iota(jnp.int32, (rows, rows), 1) // block
    same_bin = row_id == col_id
    gram = jnp.where(same_bin, gram, 0.0)
    folded = gram[:block]
    for f in range(1, FREQ_DEV):
        folded = folded + gram[f * block : (f + 1) * block]
    packed = 2 * rows <= LANES
    if packed:
        folded = jnp.concatenate([folded[:n_win], folded[n_win:]], axis=1)
    g_send[...] = folded
    g_recv[row] = folded
    for off, peer in enumerate(row_peers):
        pltpu.make_async_remote_copy(
            src_ref=g_send,
            dst_ref=g_recv.at[row],
            send_sem=g_sem.at[0],
            recv_sem=g_sem.at[1],
            device_id={"row": peer},
            device_id_type=MESH,
        ).start()
    rhs = jnp.concatenate(
        [gather(recv.at[0], number, range(n_sub, recv.shape[1])) for number in range(slab)], axis=0
    ) / math.sqrt(n_chan)
    rhs = rhs[:, :n_virt]
    for ch in range(n_chunk):
        await_all(slabs(recv, ch), send_sem.at[ch])
    for store in stores:
        store.wait()
    if n_row > 1:
        part = g_recv.at[pl.ds(0, n_row - 1)]
        pltpu.make_async_copy(part, part, g_sem.at[1]).wait()
    folded = g_recv[0]
    for other in range(1, n_row):
        folded = folded + g_recv[other]
    if packed:
        folded = jnp.concatenate([folded[:, :rows], folded[:, rows:]], axis=0)
    gram = jnp.where(same_bin, jnp.concatenate([folded] * FREQ_DEV, axis=0), 0.0)
    y_out[...] = solve(rhs, gram, FREQ_DEV, n_chan, math.sqrt(n_chan / n_win))

    if n_row > 1:
        part = g_recv.at[pl.ds(0, n_row - 1)]
        pltpu.make_async_copy(part, part, g_sem.at[0]).wait()


def expand_kernel(dims, eh, el, y, out_hbm, ov, sem):
    n_win, n_chunk, width, n_virt = dims
    block = 2 * n_win
    stores = []
    for f in range(FREQ_DEV):
        own = slice(f * block, (f + 1) * block)
        head, tail = halves(y[own, :])
        coef = jnp.concatenate([head, tail, head], axis=0)
        for ch in range(n_chunk):
            big = eh[ch, own, :]
            part = dot(coef, jnp.concatenate([big, big, el[ch, own, :]], axis=0), ((0,), (0,)))
            span = slice(ch * width, (ch + 1) * width)
            ov[f, 0, :, span] = part[:, :width]
            ov[f, 1, :, span] = part[:, width:]
        store = pltpu.make_async_copy(ov.at[f], out_hbm.at[f], sem.at[f])
        store.start()
        stores.append(store)
    for store in stores:
        store.wait()


def body(downgoing, upgoing):
    _, n_local, n_samples = downgoing.shape
    n_virt = upgoing.shape[1]
    n_win, n_row = lax.axis_size("win"), lax.axis_size("row")
    n_chan = n_local * n_row
    width = 256 if n_local % 256 == 0 else 128
    n_chunk = n_local // width
    piece = PIECE if n_samples % PIECE == 0 else n_samples
    n_piece = n_samples // piece
    slab = 2 * FREQ_DEV
    rows = n_win * slab
    block = 2 * n_win
    table = jnp.asarray(dft_table(n_samples, FREQ_DEV * n_win))
    g_shape = (n_win, 2 * rows) if 2 * rows <= LANES else (block, rows)
    v_pad = -(-n_virt // LANES) * LANES
    dims = (n_win, n_row, n_chunk, width, n_virt, n_chan)
    any_spec = pl.BlockSpec(memory_space=pl.ANY)
    vmem_spec = pl.BlockSpec(memory_space=pltpu.VMEM)
    ext = jax.ShapeDtypeStruct((n_chunk, rows, 2 * width), BF16)
    eh, el, y = pl.pallas_call(
        functools.partial(solve_kernel, dims),
        out_shape=(ext, ext, jax.ShapeDtypeStruct((rows, n_virt), F32)),
        in_specs=[pl.BlockSpec(memory_space=pltpu.MemorySpace.HBM)] * 3,
        out_specs=(any_spec, any_spec, vmem_spec),
        scratch_shapes=[
            pltpu.VMEM((n_chunk, n_piece, width, piece), F32),
            pltpu.VMEM((n_piece, n_virt, piece), F32),
            pltpu.VMEM((n_piece, piece, table.shape[1]), BF16),
            pltpu.VMEM((n_chunk, (width + v_pad) // LANES, rows, LANES), F32),
            pltpu.VMEM((n_chunk, (width + v_pad) // LANES, rows, LANES), F32),
            pltpu.VMEM((n_chunk, rows, 2 * width), BF16),
            pltpu.VMEM((n_chunk, rows, 2 * width), BF16),
            pltpu.VMEM(g_shape, F32),
            pltpu.VMEM((n_row,) + g_shape, F32),
            pltpu.SemaphoreType.DMA((n_chunk, 3 * n_piece)),
            pltpu.SemaphoreType.DMA((n_chunk,)),
            pltpu.SemaphoreType.DMA((n_chunk,)),
            pltpu.SemaphoreType.DMA((2,)),
            pltpu.SemaphoreType.DMA((2 * n_chunk,)),
        ],
        compiler_params=pltpu.CompilerParams(
            collective_id=0, has_side_effects=True, vmem_limit_bytes=50 * 1024 * 1024
        ),
        name="solve_bins",
    )(*[pltpu.with_memory_space_constraint(a, pltpu.MemorySpace.HBM) for a in (downgoing, upgoing, table)])
    out_shape = (FREQ_DEV, 2, n_virt, n_local)
    return pl.pallas_call(
        functools.partial(expand_kernel, (n_win, n_chunk, width, n_virt)),
        out_shape=jax.ShapeDtypeStruct(out_shape, F32),
        in_specs=[vmem_spec] * 3,
        out_specs=any_spec,
        scratch_shapes=[pltpu.VMEM(out_shape, F32), pltpu.SemaphoreType.DMA((FREQ_DEV,))],
        compiler_params=pltpu.CompilerParams(vmem_limit_bytes=50 * 1024 * 1024),
        name="expand_bins",
    )(eh, el, y)


def solution(mesh):
    in_specs = (P("win", "row", None), P("win", None, None))
    out_specs = P("win", None, None, "row")
    return jax.shard_map(body, mesh=mesh, in_specs=in_specs, out_specs=out_specs, check_vma=False)
```

```python
import functools
import math

import jax
import jax.numpy as jnp
import numpy as np
from jax import lax
from jax.experimental import pallas as pl
from jax.experimental.pallas import tpu as pltpu
from jax.sharding import PartitionSpec as P

FREQ_DEV = 4
PIECE = 1024
STEP = 256
ITERS = 2
DAMPING = 0.5
LANES = 128
MESH = pl.DeviceIdType.MESH
F32, BF16 = jnp.float32, jnp.bfloat16


def dft_table(n_samples, n_bins):
    angles = (np.arange(n_samples)[:, None] * np.arange(1, n_bins + 1)[None, :] % n_samples) * (
        2.0 * math.pi / n_samples
    )
    table = np.stack([np.cos(angles), -np.sin(angles)], axis=2).reshape(n_samples, 2 * n_bins)
    table = (table / math.sqrt(n_samples)).astype(np.float32)
    head = table.astype(BF16)
    tail = (table - head.astype(np.float32)).astype(BF16)
    return np.concatenate([head, tail], axis=1)


def halves(value):
    head = value.astype(BF16)
    return head, (value - head.astype(F32)).astype(BF16)


def dot(first, second, dims):
    return lax.dot_general(first, second, (dims, ((), ())), preferred_element_type=F32)


def accumulate(total, parts, table):
    for at in range(0, table.shape[0], STEP):
        span = slice(at, at + STEP)
        series = [part[:, span] for part in parts]
        series = jnp.concatenate(series, axis=0) if len(series) > 1 else series[0]
        m = series.shape[0]
        head, tail = halves(series)
        weights = table[span, :]
        part = dot(head, weights, ((1,), (0,))) + dot(tail, weights, ((1,), (0,)))
        total = part if total is None else total + part
    return total


def by_bin(total):
    m = total.shape[0]
    if m % LANES:
        total = jnp.concatenate([total, jnp.zeros((LANES - m % LANES, total.shape[1]), F32)], axis=0)
    total = total.T
    n = total.shape[0] // 2
    return total[:n] + total[n:]


def solve(rhs, gram, n_freq, n_chan, scale):
    rows, n_virt = rhs.shape

    head, tail = halves(gram)
    operator = jnp.concatenate([head, head, tail], axis=1)

    def project(coef):
        c_head, c_tail = halves(coef)
        return dot(operator, jnp.concatenate([c_head, c_tail, c_head], axis=0), ((1,), (0,)))

    def inner(one, two):
        prod = (one * two).reshape(n_freq, rows // n_freq, n_virt)
        total = jnp.sum(prod, axis=1, keepdims=True)
        return jnp.broadcast_to(total, prod.shape).reshape(rows, n_virt)

    filt = jnp.zeros_like(rhs)
    resid, direc = rhs, rhs
    resid_g = project(resid)
    direc_g = resid_g
    norm_old = inner(resid, resid_g)
    for iteration in range(ITERS):
        image = direc_g / n_chan + DAMPING * direc
        curvature = inner(direc_g, image)
        step = norm_old / curvature
        filt = filt + step * direc
        if iteration + 1 < ITERS:
            resid = resid - step * image
            resid_g = resid_g - step * project(image)
            norm_new = inner(resid, resid_g)
            ratio = norm_new / norm_old
            direc = resid + ratio * direc
            direc_g = resid_g + ratio * direc_g
            norm_old = norm_new
    return filt * scale


def solve_kernel(
    dims, x_hbm, up_hbm, tab_hbm, eh_out, el_out, y_out,
    xv, upv, tab, sbuf, recv, eh, el, g_send, g_recv,
    in_sem, send_sem, recv_sem, g_sem, out_sem,
):
    n_win, n_row, n_chunk, width, n_virt, n_chan = dims
    slab = 2 * FREQ_DEV
    rows = n_win * slab
    block = 2 * n_win
    me, row = lax.axis_index("win"), lax.axis_index("row")

    n_piece, piece = tab.shape[0], tab.shape[1]
    loads = []
    for ch in range(n_chunk):
        lines = pl.ds(ch * width, width)
        pairs = []
        for k in range(n_piece):
            span = pl.ds(k * piece, piece)
            if ch == 0:
                pairs.append((tab_hbm.at[span, :], tab.at[k]))
                pairs.append((up_hbm.at[0, :, span], upv.at[k]))
            pairs.append((x_hbm.at[0, lines, span], xv.at[ch, k]))
        loads.append(
            [
                pltpu.make_async_copy(src, dst, in_sem.at[ch, at])
                for at, (src, dst) in enumerate(pairs)
            ]
        )
    for load in loads[0]:
        load.start()

    win_peers = [lax.rem(me + off, n_win) for off in range(1, n_win)]
    row_peers = [lax.rem(row + off, n_row) for off in range(1, n_row)]
    barrier = pltpu.get_barrier_semaphore()
    for peer in win_peers:
        pl.semaphore_signal(barrier, inc=1, device_id={"win": peer}, device_id_type=MESH)
    for peer in row_peers:
        pl.semaphore_signal(barrier, inc=1, device_id={"row": peer}, device_id_type=MESH)

    n_sub = width // LANES

    def slabs(buf, ch):
        return buf.at[ch, pl.ds(0, buf.shape[1] if ch == 0 else n_sub)]

    def share(src, dst, at):
        own = pl.ds(pl.multiple_of(me * slab, slab), slab)
        dst[:, own, :] = src[:, own, :]
        for peer in win_peers:
            pltpu.make_async_remote_copy(
                src_ref=src.at[:, pl.ds(pl.multiple_of(peer * slab, slab), slab), :],
                dst_ref=dst.at[:, own, :],
                send_sem=send_sem.at[at],
                recv_sem=recv_sem.at[at],
                device_id={"win": peer},
                device_id_type=MESH,
            ).start()

    def put(dst, value):
        for sub in range(value.shape[1] // LANES):
            dst[sub] = value[:, sub * LANES : (sub + 1) * LANES]

    def gather(src, number, subs):
        parts = [src[sub, pl.ds(number, n_win, stride=slab), :] for sub in subs]
        return jnp.concatenate(parts, axis=1) if len(parts) > 1 else parts[0]

    def await_all(ref, sem):
        part = ref.at[:, pl.ds(0, (n_win - 1) * slab), :]
        pltpu.make_async_copy(part, part, sem).wait()

    for ch in range(n_chunk):
        total = None
        if ch:
            for load in loads[ch]:
                load.wait()
        for k in range(n_piece):
            for load in loads[0][3 * k : 3 * k + 3] if ch == 0 else []:
                load.wait()
            if ch == 0:
                until = k + 2 if k + 1 < n_piece else n_chunk
                for later in loads[k + 1 : until]:
                    for load in later:
                        load.start()
            parts = [xv.at[ch, k]] + ([upv.at[k]] if ch == 0 else [])
            total = accumulate(total, parts, tab.at[k])
        put(sbuf.at[ch], by_bin(total))
        if ch == 0:
            pl.semaphore_wait(barrier, n_win + n_row - 2)
        share(slabs(sbuf, ch), slabs(recv, ch), ch)

    gram = None
    stores = []
    for ch in range(n_chunk):
        await_all(slabs(recv, ch), recv_sem.at[ch])
        left, right = [], []
        for f in range(FREQ_DEV):
            real = gather(recv.at[ch], 2 * f, range(n_sub))
            imag = gather(recv.at[ch], 2 * f + 1, range(n_sub))
            left += [real, imag]
            right += [-imag, real]
        ext = jnp.concatenate(
            [jnp.concatenate(left, axis=0), jnp.concatenate(right, axis=0)], axis=1
        )
        head, tail = halves(ext)
        eh[ch] = head
        el[ch] = tail
        for number, (src, dst) in enumerate(((eh, eh_out), (el, el_out))):
            store = pltpu.make_async_copy(src.at[ch], dst.at[ch], out_sem.at[2 * ch + number])
            store.start()
            stores.append(store)
        part = dot(
            jnp.concatenate([head, head, tail], axis=1),
            jnp.concatenate([head, tail, head], axis=1),
            ((1,), (1,)),
        )
        gram = part if gram is None else gram + part

    row_id = lax.broadcasted_iota(jnp.int32, (rows, rows), 0) // block
    col_id = lax.broadcasted_iota(jnp.int32, (rows, rows), 1) // block
    same_bin = row_id == col_id
    gram = jnp.where(same_bin, gram, 0.0)
    folded = gram[:block]
    for f in range(1, FREQ_DEV):
        folded = folded + gram[f * block : (f + 1) * block]
    packed = 2 * rows <= LANES
    if packed:
        folded = jnp.concatenate([folded[:n_win], folded[n_win:]], axis=1)
    g_send[...] = folded
    g_recv[row] = folded
    for off, peer in enumerate(row_peers):
        pltpu.make_async_remote_copy(
            src_ref=g_send,
            dst_ref=g_recv.at[row],
            send_sem=g_sem.at[0],
            recv_sem=g_sem.at[1],
            device_id={"row": peer},
            device_id_type=MESH,
        ).start()
    rhs = jnp.concatenate(
        [gather(recv.at[0], number, range(n_sub, recv.shape[1])) for number in range(slab)], axis=0
    ) / math.sqrt(n_chan)
    rhs = rhs[:, :n_virt]
    for ch in range(n_chunk):
        await_all(slabs(recv, ch), send_sem.at[ch])
    for store in stores:
        store.wait()
    if n_row > 1:
        part = g_recv.at[pl.ds(0, n_row - 1)]
        pltpu.make_async_copy(part, part, g_sem.at[1]).wait()
    folded = g_recv[0]
    for other in range(1, n_row):
        folded = folded + g_recv[other]
    if packed:
        folded = jnp.concatenate([folded[:, :rows], folded[:, rows:]], axis=0)
    gram = jnp.where(same_bin, jnp.concatenate([folded] * FREQ_DEV, axis=0), 0.0)
    y_out[...] = solve(rhs, gram, FREQ_DEV, n_chan, math.sqrt(n_chan / n_win))

    if n_row > 1:
        part = g_recv.at[pl.ds(0, n_row - 1)]
        pltpu.make_async_copy(part, part, g_sem.at[0]).wait()


def expand_kernel(dims, eh, el, y, out_hbm, ov, sem):
    n_win, n_chunk, width, n_virt = dims
    block = 2 * n_win
    stores = []
    for f in range(FREQ_DEV):
        own = slice(f * block, (f + 1) * block)
        head, tail = halves(y[own, :])
        coef = jnp.concatenate([head, tail, head], axis=0)
        for ch in range(n_chunk):
            big = eh[ch, own, :]
            part = dot(coef, jnp.concatenate([big, big, el[ch, own, :]], axis=0), ((0,), (0,)))
            span = slice(ch * width, (ch + 1) * width)
            ov[f, 0, :, span] = part[:, :width]
            ov[f, 1, :, span] = part[:, width:]
        store = pltpu.make_async_copy(ov.at[f], out_hbm.at[f], sem.at[f])
        store.start()
        stores.append(store)
    for store in stores:
        store.wait()


def body(downgoing, upgoing):
    _, n_local, n_samples = downgoing.shape
    n_virt = upgoing.shape[1]
    n_win, n_row = lax.axis_size("win"), lax.axis_size("row")
    n_chan = n_local * n_row
    width = next(w for w in (384, 256, 128) if n_local % w == 0)
    n_chunk = n_local // width
    piece = PIECE if n_samples % PIECE == 0 else n_samples
    n_piece = n_samples // piece
    slab = 2 * FREQ_DEV
    rows = n_win * slab
    block = 2 * n_win
    table = jnp.asarray(dft_table(n_samples, FREQ_DEV * n_win))
    g_shape = (n_win, 2 * rows) if 2 * rows <= LANES else (block, rows)
    v_pad = -(-n_virt // LANES) * LANES
    dims = (n_win, n_row, n_chunk, width, n_virt, n_chan)
    any_spec = pl.BlockSpec(memory_space=pl.ANY)
    vmem_spec = pl.BlockSpec(memory_space=pltpu.VMEM)
    ext = jax.ShapeDtypeStruct((n_chunk, rows, 2 * width), BF16)
    eh, el, y = pl.pallas_call(
        functools.partial(solve_kernel, dims),
        out_shape=(ext, ext, jax.ShapeDtypeStruct((rows, n_virt), F32)),
        in_specs=[pl.BlockSpec(memory_space=pltpu.MemorySpace.HBM)] * 3,
        out_specs=(any_spec, any_spec, vmem_spec),
        scratch_shapes=[
            pltpu.VMEM((n_chunk, n_piece, width, piece), F32),
            pltpu.VMEM((n_piece, n_virt, piece), F32),
            pltpu.VMEM((n_piece, piece, table.shape[1]), BF16),
            pltpu.VMEM((n_chunk, (width + v_pad) // LANES, rows, LANES), F32),
            pltpu.VMEM((n_chunk, (width + v_pad) // LANES, rows, LANES), F32),
            pltpu.VMEM((n_chunk, rows, 2 * width), BF16),
            pltpu.VMEM((n_chunk, rows, 2 * width), BF16),
            pltpu.VMEM(g_shape, F32),
            pltpu.VMEM((n_row,) + g_shape, F32),
            pltpu.SemaphoreType.DMA((n_chunk, 3 * n_piece)),
            pltpu.SemaphoreType.DMA((n_chunk,)),
            pltpu.SemaphoreType.DMA((n_chunk,)),
            pltpu.SemaphoreType.DMA((2,)),
            pltpu.SemaphoreType.DMA((2 * n_chunk,)),
        ],
        compiler_params=pltpu.CompilerParams(
            collective_id=0, has_side_effects=True, vmem_limit_bytes=50 * 1024 * 1024
        ),
        name="solve_bins",
    )(*[pltpu.with_memory_space_constraint(a, pltpu.MemorySpace.HBM) for a in (downgoing, upgoing, table)])
    out_shape = (FREQ_DEV, 2, n_virt, n_local)
    return pl.pallas_call(
        functools.partial(expand_kernel, (n_win, n_chunk, width, n_virt)),
        out_shape=jax.ShapeDtypeStruct(out_shape, F32),
        in_specs=[vmem_spec] * 3,
        out_specs=any_spec,
        scratch_shapes=[pltpu.VMEM(out_shape, F32), pltpu.SemaphoreType.DMA((FREQ_DEV,))],
        compiler_params=pltpu.CompilerParams(vmem_limit_bytes=50 * 1024 * 1024),
        name="expand_bins",
    )(eh, el, y)


def solution(mesh):
    in_specs = (P("win", "row", None), P("win", None, None))
    out_specs = P("win", None, None, "row")
    return jax.shard_map(body, mesh=mesh, in_specs=in_specs, out_specs=out_specs, check_vma=False)
```

```python
import functools
import math

import jax
import jax.numpy as jnp
import numpy as np
from jax import lax
from jax.experimental import pallas as pl
from jax.experimental.pallas import tpu as pltpu
from jax.sharding import PartitionSpec as P

FREQ_DEV = 4
PIECE = 1024
STEP = 256
ITERS = 2
DAMPING = 0.5
LANES = 128
MESH = pl.DeviceIdType.MESH
F32, BF16 = jnp.float32, jnp.bfloat16


def dft_table(n_samples, n_bins):
    angles = (np.arange(n_samples)[:, None] * np.arange(1, n_bins + 1)[None, :] % n_samples) * (
        2.0 * math.pi / n_samples
    )
    table = np.stack([np.cos(angles), -np.sin(angles)], axis=2).reshape(n_samples, 2 * n_bins)
    table = (table / math.sqrt(n_samples)).astype(np.float32)
    head = table.astype(BF16)
    tail = (table - head.astype(np.float32)).astype(BF16)
    return np.concatenate([head, tail], axis=1)


def halves(value):
    head = value.astype(BF16)
    return head, (value - head.astype(F32)).astype(BF16)


def dot(first, second, dims):
    return lax.dot_general(first, second, (dims, ((), ())), preferred_element_type=F32)


def accumulate(total, parts, table):
    for at in range(0, table.shape[0], STEP):
        span = slice(at, at + STEP)
        series = [part[:, span] for part in parts]
        series = jnp.concatenate(series, axis=0) if len(series) > 1 else series[0]
        m = series.shape[0]
        head, tail = halves(series)
        weights = table[span, :]
        part = dot(head, weights, ((1,), (0,))) + dot(tail, weights, ((1,), (0,)))
        total = part if total is None else total + part
    return total


def by_bin(total):
    m = total.shape[0]
    if m % LANES:
        total = jnp.concatenate([total, jnp.zeros((LANES - m % LANES, total.shape[1]), F32)], axis=0)
    total = total.T
    n = total.shape[0] // 2
    return total[:n] + total[n:]


def solve(rhs, gram, n_freq, n_chan, scale):
    rows, n_virt = rhs.shape

    head, tail = halves(gram)
    operator = jnp.concatenate([head, head, tail], axis=1)

    def project(coef):
        c_head, c_tail = halves(coef)
        return dot(operator, jnp.concatenate([c_head, c_tail, c_head], axis=0), ((1,), (0,)))

    def inner(one, two):
        prod = (one * two).reshape(n_freq, rows // n_freq, n_virt)
        total = jnp.sum(prod, axis=1, keepdims=True)
        return jnp.broadcast_to(total, prod.shape).reshape(rows, n_virt)

    filt = jnp.zeros_like(rhs)
    resid, direc = rhs, rhs
    resid_g = project(resid)
    direc_g = resid_g
    norm_old = inner(resid, resid_g)
    for iteration in range(ITERS):
        image = direc_g / n_chan + DAMPING * direc
        curvature = inner(direc_g, image)
        step = norm_old / curvature
        filt = filt + step * direc
        if iteration + 1 < ITERS:
            resid = resid - step * image
            resid_g = resid_g - step * project(image)
            norm_new = inner(resid, resid_g)
            ratio = norm_new / norm_old
            direc = resid + ratio * direc
            direc_g = resid_g + ratio * direc_g
            norm_old = norm_new
    return filt * scale


def solve_kernel(
    dims, x_hbm, up_hbm, tab_hbm, eh_out, el_out, y_out,
    xv, upv, tab, sbuf, recv, eh, el, g_send, g_recv,
    in_sem, send_sem, recv_sem, g_sem, out_sem,
):
    n_win, n_row, n_chunk, width, n_virt, n_chan = dims
    slab = 2 * FREQ_DEV
    rows = n_win * slab
    block = 2 * n_win
    me, row = lax.axis_index("win"), lax.axis_index("row")

    n_piece, piece = tab.shape[0], tab.shape[1]
    loads = []
    for ch in range(n_chunk):
        lines = pl.ds(ch * width, width)
        pairs = []
        for k in range(n_piece):
            span = pl.ds(k * piece, piece)
            if ch == 0:
                pairs.append((tab_hbm.at[span, :], tab.at[k]))
                pairs.append((up_hbm.at[0, :, span], upv.at[k]))
            pairs.append((x_hbm.at[0, lines, span], xv.at[ch, k]))
        loads.append(
            [
                pltpu.make_async_copy(src, dst, in_sem.at[ch, at])
                for at, (src, dst) in enumerate(pairs)
            ]
        )
    for load in loads[0]:
        load.start()

    win_peers = [lax.rem(me + off, n_win) for off in range(1, n_win)]
    row_peers = [lax.rem(row + off, n_row) for off in range(1, n_row)]
    barrier = pltpu.get_barrier_semaphore()
    for peer in win_peers:
        pl.semaphore_signal(barrier, inc=1, device_id={"win": peer}, device_id_type=MESH)
    for peer in row_peers:
        pl.semaphore_signal(barrier, inc=1, device_id={"row": peer}, device_id_type=MESH)

    n_sub = width // LANES

    def slabs(buf, ch):
        return buf.at[ch, pl.ds(0, buf.shape[1] if ch == 0 else n_sub)]

    def share(src, dst, at):
        own = pl.ds(pl.multiple_of(me * slab, slab), slab)
        dst[:, own, :] = src[:, own, :]
        for peer in win_peers:
            pltpu.make_async_remote_copy(
                src_ref=src.at[:, pl.ds(pl.multiple_of(peer * slab, slab), slab), :],
                dst_ref=dst.at[:, own, :],
                send_sem=send_sem.at[at],
                recv_sem=recv_sem.at[at],
                device_id={"win": peer},
                device_id_type=MESH,
            ).start()

    def put(dst, value):
        for sub in range(value.shape[1] // LANES):
            dst[sub] = value[:, sub * LANES : (sub + 1) * LANES]

    def gather(src, number, subs):
        parts = [src[sub, pl.ds(number, n_win, stride=slab), :] for sub in subs]
        return jnp.concatenate(parts, axis=1) if len(parts) > 1 else parts[0]

    def await_all(ref, sem):
        part = ref.at[:, pl.ds(0, (n_win - 1) * slab), :]
        pltpu.make_async_copy(part, part, sem).wait()

    for ch in range(n_chunk):
        total = None
        if ch:
            for load in loads[ch]:
                load.wait()
        for k in range(n_piece):
            for load in loads[0][3 * k : 3 * k + 3] if ch == 0 else []:
                load.wait()
            if ch == 0:
                until = k + 2 if k + 1 < n_piece else n_chunk
                for later in loads[k + 1 : until]:
                    for load in later:
                        load.start()
            parts = [xv.at[ch, k]] + ([upv.at[k]] if ch == 0 else [])
            total = accumulate(total, parts, tab.at[k])
        put(sbuf.at[ch], by_bin(total))
        if ch == 0:
            pl.semaphore_wait(barrier, n_win + n_row - 2)
        share(slabs(sbuf, ch), slabs(recv, ch), ch)

    gram = None
    stores = []
    for ch in range(n_chunk):
        await_all(slabs(recv, ch), recv_sem.at[ch])
        left, right = [], []
        for f in range(FREQ_DEV):
            real = gather(recv.at[ch], 2 * f, range(n_sub))
            imag = gather(recv.at[ch], 2 * f + 1, range(n_sub))
            left += [real, imag]
            right += [-imag, real]
        ext = jnp.concatenate(
            [jnp.concatenate(left, axis=0), jnp.concatenate(right, axis=0)], axis=1
        )
        head, tail = halves(ext)
        eh[ch] = head
        el[ch] = tail
        for number, (src, dst) in enumerate(((eh, eh_out), (el, el_out))):
            store = pltpu.make_async_copy(src.at[ch], dst.at[ch], out_sem.at[2 * ch + number])
            store.start()
            stores.append(store)
        part = dot(
            jnp.concatenate([head, head, tail], axis=1),
            jnp.concatenate([head, tail, head], axis=1),
            ((1,), (1,)),
        )
        gram = part if gram is None else gram + part

    row_id = lax.broadcasted_iota(jnp.int32, (rows, rows), 0) // block
    col_id = lax.broadcasted_iota(jnp.int32, (rows, rows), 1) // block
    same_bin = row_id == col_id
    gram = jnp.where(same_bin, gram, 0.0)
    folded = gram[:block]
    for f in range(1, FREQ_DEV):
        folded = folded + gram[f * block : (f + 1) * block]
    packed = 2 * rows <= LANES
    if packed:
        folded = jnp.concatenate([folded[:n_win], folded[n_win:]], axis=1)
    g_send[...] = folded
    g_recv[row] = folded
    for off, peer in enumerate(row_peers):
        pltpu.make_async_remote_copy(
            src_ref=g_send,
            dst_ref=g_recv.at[row],
            send_sem=g_sem.at[0],
            recv_sem=g_sem.at[1],
            device_id={"row": peer},
            device_id_type=MESH,
        ).start()
    rhs = jnp.concatenate(
        [gather(recv.at[0], number, range(n_sub, recv.shape[1])) for number in range(slab)], axis=0
    ) / math.sqrt(n_chan)
    rhs = rhs[:, :n_virt]
    for ch in range(n_chunk):
        await_all(slabs(recv, ch), send_sem.at[ch])
    for store in stores:
        store.wait()
    if n_row > 1:
        part = g_recv.at[pl.ds(0, n_row - 1)]
        pltpu.make_async_copy(part, part, g_sem.at[1]).wait()
    folded = g_recv[0]
    for other in range(1, n_row):
        folded = folded + g_recv[other]
    if packed:
        folded = jnp.concatenate([folded[:, :rows], folded[:, rows:]], axis=0)
    gram = jnp.where(same_bin, jnp.concatenate([folded] * FREQ_DEV, axis=0), 0.0)
    y_out[...] = solve(rhs, gram, FREQ_DEV, n_chan, math.sqrt(n_chan / n_win))

    if n_row > 1:
        part = g_recv.at[pl.ds(0, n_row - 1)]
        pltpu.make_async_copy(part, part, g_sem.at[0]).wait()


def expand_kernel(dims, eh, el, y, out_hbm, ov, sem):
    n_win, n_chunk, width, n_virt = dims
    block = 2 * n_win
    stores = []
    for f in range(FREQ_DEV):
        own = slice(f * block, (f + 1) * block)
        head, tail = halves(y[own, :])
        coef = jnp.concatenate([head, tail, head], axis=0)
        for ch in range(n_chunk):
            big = eh[ch, own, :]
            part = dot(coef, jnp.concatenate([big, big, el[ch, own, :]], axis=0), ((0,), (0,)))
            span = slice(ch * width, (ch + 1) * width)
            ov[f, 0, :, span] = part[:, :width]
            ov[f, 1, :, span] = part[:, width:]
        store = pltpu.make_async_copy(ov.at[f], out_hbm.at[f], sem.at[f])
        store.start()
        stores.append(store)
    for store in stores:
        store.wait()


def body(downgoing, upgoing):
    _, n_local, n_samples = downgoing.shape
    n_virt = upgoing.shape[1]
    n_win, n_row = lax.axis_size("win"), lax.axis_size("row")
    n_chan = n_local * n_row
    width = 128
    n_chunk = n_local // width
    piece = PIECE if n_samples % PIECE == 0 else n_samples
    n_piece = n_samples // piece
    slab = 2 * FREQ_DEV
    rows = n_win * slab
    block = 2 * n_win
    table = jnp.asarray(dft_table(n_samples, FREQ_DEV * n_win))
    g_shape = (n_win, 2 * rows) if 2 * rows <= LANES else (block, rows)
    v_pad = -(-n_virt // LANES) * LANES
    dims = (n_win, n_row, n_chunk, width, n_virt, n_chan)
    any_spec = pl.BlockSpec(memory_space=pl.ANY)
    vmem_spec = pl.BlockSpec(memory_space=pltpu.VMEM)
    ext = jax.ShapeDtypeStruct((n_chunk, rows, 2 * width), BF16)
    eh, el, y = pl.pallas_call(
        functools.partial(solve_kernel, dims),
        out_shape=(ext, ext, jax.ShapeDtypeStruct((rows, n_virt), F32)),
        in_specs=[pl.BlockSpec(memory_space=pltpu.MemorySpace.HBM)] * 3,
        out_specs=(any_spec, any_spec, vmem_spec),
        scratch_shapes=[
            pltpu.VMEM((n_chunk, n_piece, width, piece), F32),
            pltpu.VMEM((n_piece, n_virt, piece), F32),
            pltpu.VMEM((n_piece, piece, table.shape[1]), BF16),
            pltpu.VMEM((n_chunk, (width + v_pad) // LANES, rows, LANES), F32),
            pltpu.VMEM((n_chunk, (width + v_pad) // LANES, rows, LANES), F32),
            pltpu.VMEM((n_chunk, rows, 2 * width), BF16),
            pltpu.VMEM((n_chunk, rows, 2 * width), BF16),
            pltpu.VMEM(g_shape, F32),
            pltpu.VMEM((n_row,) + g_shape, F32),
            pltpu.SemaphoreType.DMA((n_chunk, 3 * n_piece)),
            pltpu.SemaphoreType.DMA((n_chunk,)),
            pltpu.SemaphoreType.DMA((n_chunk,)),
            pltpu.SemaphoreType.DMA((2,)),
            pltpu.SemaphoreType.DMA((2 * n_chunk,)),
        ],
        compiler_params=pltpu.CompilerParams(
            collective_id=0, has_side_effects=True, vmem_limit_bytes=50 * 1024 * 1024
        ),
        name="solve_bins",
    )(*[pltpu.with_memory_space_constraint(a, pltpu.MemorySpace.HBM) for a in (downgoing, upgoing, table)])
    out_shape = (FREQ_DEV, 2, n_virt, n_local)
    return pl.pallas_call(
        functools.partial(expand_kernel, (n_win, n_chunk, width, n_virt)),
        out_shape=jax.ShapeDtypeStruct(out_shape, F32),
        in_specs=[vmem_spec] * 3,
        out_specs=any_spec,
        scratch_shapes=[pltpu.VMEM(out_shape, F32), pltpu.SemaphoreType.DMA((FREQ_DEV,))],
        compiler_params=pltpu.CompilerParams(vmem_limit_bytes=50 * 1024 * 1024),
        name="expand_bins",
    )(eh, el, y)


def solution(mesh):
    in_specs = (P("win", "row", None), P("win", None, None))
    out_specs = P("win", None, None, "row")
    return jax.shard_map(body, mesh=mesh, in_specs=in_specs, out_specs=out_specs, check_vma=False)
```
